512 devices in a mesh: blk: 64 (over x, y, z_hi, core), row: 8 (over z_lo).
Axes of the slice: x: 4, y: 4, z: 16 (z_hi: 2, z_lo: 8; z = z_hi * 8 + z_lo), core: 2. Of those that a mesh axis runs over, the one named last changes fastest.
Arguments:
- amplitudes: bfloat16 [1152, 4, 1152], P('blk', None, 'row'), may hold values from -6 to 6
- cholesky: bfloat16 [64, 1152, 1152], P('blk'), may hold values from -0.109375 to 0.109375
- virt_irreps: int32 [1152], replicated, may hold values from 0 to 7, as said below
- pair_irreps: int32 [4], replicated, may hold values from 0 to 7
Outputs:
- ladder_sigma: bfloat16 [1152, 4, 1152], P('blk', None, 'row')
The draws below stay inside these ranges and needn't reach their ends.
Inputs may be any that keep to these rules, and one draw needn't show every extreme that they name: `virt_irreps`: irreps of two orbitals combine by exclusive or; in each aligned block of 144 virtual orbitals no irrep holds more than 36 orbitals, and one irrep holds exactly 36. `pair_irreps`: one irrep per pair of the slab.
All inputs are finite; a program needn't handle non-finite values.
Results may differ from the reference program's by a relative error of at most 0.0049.
Values may be sent and summed in bfloat16 or wider, within the bound.
A program may use at most 64 MiB of HBM per device.

```python
import jax
import jax.numpy as jnp
from jax import lax

NV = 1152
PAIRS = 4
NQ = 64
CAP = 36
N_ROW = 8


def draw_virt_irreps(key, part):
    key = jax.random.fold_in(key, 11)
    block_len = NV // N_ROW
    most = CAP
    keys = jax.random.split(key, N_ROW)

    def one_block(block_key):
        first_key, second_key, third_key = jax.random.split(block_key, 3)
        common = jax.random.randint(first_key, (), 0, 8)
        spread = jax.random.permutation(second_key, block_len - most) % 7
        others = (common + 1 + spread) % 8
        values = jnp.concatenate([jnp.full((most,), common, jnp.int32), others.astype(jnp.int32)])
        order = jax.random.permutation(third_key, block_len)
        return values[order]
    return jax.vmap(one_block)(keys).reshape(NV).astype(jnp.int32)


def set_ends(drawn, key, least, top_value):
    longest = drawn.shape.index(max(drawn.shape))
    spots = []
    for shift in (0, 1):
        where = [jax.random.randint(jax.random.fold_in(key, axis), (), 0, length) for axis, length in enumerate(drawn.shape)]
        where[longest] = (where[longest] + shift) % drawn.shape[longest]
        spots.append(tuple(where))
    return drawn.at[spots[0]].set(least).at[spots[1]].set(top_value)


def block_scale(own_key, shape, cuts, low, high):
    loudness = 1.0
    for axis_at, shards_of in cuts:
        heights = jax.random.uniform(jax.random.fold_in(jax.random.fold_in(own_key, 6), axis_at), (shards_of,), jnp.float32, low / len(cuts), high / len(cuts))
        loudness = loudness * jnp.repeat(jnp.exp(heights), shape[axis_at] // shards_of).reshape((-1,) + (1,) * (len(shape) - 1 - axis_at))
    return loudness


def centred(stream_key, extent, width, most, shards=(), dtype=jnp.bfloat16):
    array = width * jax.random.normal(stream_key, extent, jnp.float32)
    if shards:
        array = array * block_scale(stream_key, extent, shards, -0.22, 0.18)
    return jnp.clip(array, -most, most).astype(dtype)


def setup_inputs(seed: int = 0) -> dict:
    splits = jax.random.split(jax.random.key(seed), 5)
    amplitudes = centred(splits[0], (NV, PAIRS, NV), 1.0, 6.0, ((0, 64), (2, 8)))
    cholesky = centred(splits[1], (NQ, NV, NV), (NV * 3) ** -0.5, 0.109375, ((0, 64),))
    virt_irreps = draw_virt_irreps(jax.random.fold_in(splits[4], 71), 0)
    pair_irreps = set_ends(jax.random.randint(splits[3], (PAIRS,), 0, 8), jax.random.fold_in(splits[3], 1), 0, 7).astype(jnp.int32)
    return dict(amplitudes=amplitudes, cholesky=cholesky, virt_irreps=virt_irreps, pair_irreps=pair_irreps)


def allowed(irrep_rows, irrep_cols, pair_irreps):
    product = jnp.bitwise_xor(irrep_rows[:, None, None], irrep_cols[None, None, :])
    return product == pair_irreps[None, :, None]


def reference(amplitudes, cholesky, virt_irreps, pair_irreps):
    allowed_in = allowed(virt_irreps, virt_irreps, pair_irreps)
    projected = jnp.where(allowed_in, amplitudes, jnp.zeros_like(amplitudes)).astype(jnp.float32)

    def add_vector(running, vectors):
        factor = vectors.astype(jnp.float32)
        contracted = jnp.einsum("dpc,ac->dpa", projected, factor).astype(jnp.bfloat16)
        contracted = lax.optimization_barrier(contracted)
        addend = jnp.einsum("bd,dpa->bpa", factor, contracted.astype(jnp.float32))
        return running + addend, None

    running, unused = lax.scan(add_vector, jnp.zeros(amplitudes.shape, jnp.float32), cholesky)
    return jnp.where(allowed_in, running, jnp.zeros_like(running)).astype(jnp.bfloat16)
```

```python
import jax
import jax.numpy as jnp
from jax import lax
from jax.experimental import pallas as pl
from jax.experimental.pallas import tpu as pltpu
from jax.sharding import PartitionSpec as P

NV = 1152
BLK = 144
TILE = 18
HALF = 576
CHIP = 72
ROW4 = 288
F32 = jnp.float32
BF16 = jnp.bfloat16
I32 = jnp.int32
MESH = pl.DeviceIdType.MESH


def iota(shape, dim):
    return lax.broadcasted_iota(I32, shape, dim)


def dot(a, b):
    return jnp.dot(a, b, preferred_element_type=F32)


def dot_nt(a, b):
    return lax.dot_general(a, b, (((1,), (1,)), ((), ())), preferred_element_type=F32)


def lane_key(lane):
    main = ((lane >> 5) << 6) + (lane & 31)
    tail = (((lane >> 2) & 3) << 6) + 32 + (lane & 3)
    return jnp.where(lane < 128, main, tail)


def over36(v):
    return (v >= 36).astype(I32) + (v >= 72).astype(I32) + (v >= 108).astype(I32)


def kernel(
    amp_ref, chol_ref, irr_ref, pair_ref, out_ref,
    vec, irrblk, rankblk, irrhalf, rankrow, rankhalf, colg, x32, own, rpack,
    lanek, expand, reduce_r, tailsel, tx1, rx1, gathered, texp, inner, outgoing,
    sibling, summed, rx3, tx4, rx4,
    vec_sem, s1_send, s1_recv, s2_send, s2_fwd, s2_recv, s3_sib_send, s3_sib_recv,
    s3_send, s3_recv, s4_send, s4_recv,
):
    j = lax.axis_index("blk")
    r = lax.axis_index("row")
    m, zh, core = j // 4, (j // 2) % 2, j % 2
    x, y = m // 4, m % 4
    p, h = r // 2, r % 2
    other = 4 * m + 2 * zh + (1 - core)

    load_vec = pltpu.make_async_copy(chol_ref.at[0], vec, vec_sem)
    load_vec.start()

    barrier = pltpu.get_barrier_semaphore()

    def greet_line(t, c):
        @pl.when(jnp.logical_or(t // 8 != 2 * zh + core, t % 8 != r))
        def _():
            pl.semaphore_signal(barrier, inc=1, device_id=(4 * m + t // 8, t % 8), device_id_type=MESH)
        return c

    lax.fori_loop(0, 32, greet_line, 0)

    def peer(o):
        return 4 * ((x + o // 4) % 4) + (y + o) % 4

    def source(o):
        return 4 * ((x + 4 - o // 4) % 4) + (y + 4 - o % 4) % 4

    def greet_plane(o, c):
        pl.semaphore_signal(barrier, inc=1, device_id=(4 * peer(o) + 2 * zh + core, r), device_id_type=MESH)
        return c

    lax.fori_loop(1, 16, greet_plane, 0)

    irr = irr_ref[...]
    upper = (iota((BLK, BLK), 0) < iota((BLK, BLK), 1)).astype(BF16)
    eye = iota((BLK, BLK), 0) == iota((BLK, BLK), 1)
    ones = jnp.ones((BLK, 128), BF16)
    pair_own = pair_ref[p]
    members = []
    for b in range(8):
        irr_b = irr[:, BLK * b : BLK * (b + 1)]
        irrblk[b : b + 1, :] = irr_b
        members.append((jnp.broadcast_to(irr_b, (8, BLK)) == iota((8, BLK), 0)).astype(F32))
        diagonal = jnp.where(eye, jnp.broadcast_to(irr_b, (BLK, BLK)), 0).astype(F32).astype(BF16)
        column = dot(diagonal, ones).astype(I32)
        colg[BLK * b : BLK * (b + 1), :] = jnp.bitwise_xor(column, pair_own)
    irrhalf[0:1, :] = irr[:, :HALF]
    irrhalf[1:2, :] = irr[:, HALF:]
    members = jnp.concatenate(members, axis=0)
    before = members * dot(members.astype(BF16), upper)
    for b in range(8):
        rank_b = jnp.sum(before[8 * b : 8 * b + 8], axis=0, keepdims=True).astype(I32)
        rankblk[b : b + 1, :] = rank_b
        keyed = rank_b + 64 * b
        rankrow[:, BLK * b : BLK * (b + 1)] = keyed
    rankhalf[0:1, :] = rankrow[:, :HALF]
    rankhalf[1:2, :] = rankrow[:, HALF:] - 256

    row72 = iota((CHIP, 1), 0)
    own_index = TILE * j + (row72 >> 2)
    own_irr = jnp.sum(
        jnp.where(iota((CHIP, NV), 1) == own_index, jnp.broadcast_to(irr, (CHIP, NV)), 0).astype(F32),
        axis=1, keepdims=True,
    ).astype(I32)
    pairs_col = jnp.zeros((CHIP, 1), I32)
    for q in range(4):
        pairs_col = jnp.where((row72 & 3) == q, pair_ref[q], pairs_col)
    own_goal = jnp.bitwise_xor(own_irr, pairs_col)
    own_mask = (own_goal == irrblk[pl.ds(r, 1), :]).astype(F32)
    own[...] = own_mask
    lane128 = iota((128, BLK), 0)
    slot128 = lane128 - 36 * over36(lane128)
    rpack[...] = jnp.logical_and(lane128 < 108, slot128 == rankblk[pl.ds(r, 1), :]).astype(BF16)
    for dd in range(TILE):
        x32[4 * dd : 4 * dd + 4, :] = amp_ref[dd].astype(F32)
    masked = (x32[...] * own_mask).astype(BF16)
    lane_group = over36(iota((CHIP, 128), 1))
    third = iota((CHIP, 128), 0)
    third = (third >= 24).astype(I32) + (third >= 48).astype(I32)
    spread = jnp.where(lane_group == third, dot_nt(masked, rpack[...]), 0.0).astype(BF16)
    pk_row, pk_col = iota((32, CHIP), 0), iota((32, CHIP), 1)
    col_third = (pk_col >= 24).astype(I32) + (pk_col >= 48).astype(I32)
    pick = jnp.logical_and(
        (pk_row >> 3) == (pk_col & 3), (pk_row & 7) == (pk_col >> 2) - 6 * col_third
    ).astype(BF16)
    packed = dot(pick, spread)
    for q in range(4):
        tx1[q] = packed[8 * q : 8 * q + 8]

    pl.semaphore_wait(barrier, 46)

    slot_me = (r % 4) * 4 + 2 * zh + core

    def s1_copy(t):
        return pltpu.make_async_remote_copy(
            src_ref=tx1.at[(t % 8) // 2], dst_ref=rx1.at[slot_me],
            send_sem=s1_send.at[t], recv_sem=s1_recv,
            device_id=(4 * m + 2 * (t // 8) + r // 4, t % 8), device_id_type=MESH,
        )

    def s1_is_me(t):
        return jnp.logical_and(core == r // 4, jnp.logical_and(t // 8 == zh, t % 8 == r))

    def s1_start(t, c):
        me = s1_is_me(t)

        @pl.when(jnp.logical_not(me))
        def _():
            s1_copy(t).start()

        @pl.when(me)
        def _():
            pltpu.make_async_copy(tx1.at[p], rx1.at[slot_me], s1_recv).start()
        return c

    lax.fori_loop(0, 16, s1_start, 0)

    col = iota((1, 768), 1)
    key = lane_key(col & 255)
    target = (key >> 6) * 128 + 36 * (col >> 8) + (key & 63)
    lanek[...] = (iota((512, 768), 0) == target).astype(BF16)
    lane_col = iota((512, 1), 0)
    expand[...] = (lane_key(lane_col & 255) + 256 * (lane_col >> 8) == rankrow[...]).astype(BF16)
    reduce_r[...] = (lane_key(iota((256, 1), 0)) == rankhalf[pl.ds(h, 1), :]).astype(BF16)
    ts_row, ts_col = iota((320, 64), 0), iota((320, 64), 1)
    tailsel[...] = jnp.logical_and(
        (ts_row >> 3) == 10 * (ts_col >> 4) + (ts_col & 15), (ts_col & 15) < 10
    ).astype(BF16)
    u_row, u_lane = iota((ROW4, 128), 0), iota((ROW4, 128), 1)
    u_match = (u_row & 7) == (u_lane >> 4)
    u_match320 = (iota((320, 128), 0) & 7) == (iota((320, 128), 1) >> 4)

    def row_target(c):
        return TILE * ((c >> 3) & 3) + 6 * (c >> 5) + (c & 7)

    rs_row, rs_col = iota((80, 96), 0), iota((80, 96), 1)
    rowsel = jnp.logical_and(rs_row == row_target(rs_col), (rs_col & 7) < 6).astype(BF16)
    rt_row, rt_col = iota((96, 80), 0), iota((96, 80), 1)
    rowsel_t = jnp.logical_and(rt_col == row_target(rt_row), (rt_row & 7) < 6).astype(BF16)
    tail_pack = ((iota((16, 80), 1) >> 3) == iota((16, 80), 0)).astype(BF16)
    tp_row, tp_col = iota((64, ROW4), 0), iota((64, ROW4), 1)
    tail_pack4 = jnp.logical_and(
        (tp_col >> 3) == 9 * (tp_row >> 4) + (tp_row & 15), (tp_row & 15) < 9
    ).astype(BF16)

    pltpu.make_async_copy(rx1, rx1, s1_recv).wait()
    arrived = jnp.concatenate([rx1[s] for s in range(16)], axis=0)
    wide = jnp.concatenate([arrived[32 * g : 32 * g + 32] for g in range(4)], axis=1).astype(BF16)
    placed = dot(wide, lanek[...]).astype(BF16)
    stacked = jnp.concatenate([placed[:, 256 * k : 256 * k + 256] for k in range(3)], axis=0)
    rows = dot(rowsel, stacked)
    gathered[core, m, 0:80] = rows[:, :128].astype(BF16)
    tails = jnp.where(u_match320[:80], rows[:, 128:], 0.0).astype(BF16)
    gathered[core, m, 80:96] = dot(tail_pack, tails).astype(BF16)

    def s2_copy(o):
        return pltpu.make_async_remote_copy(
            src_ref=gathered.at[core, m], dst_ref=gathered.at[core, m],
            send_sem=s2_send.at[o], recv_sem=s2_recv.at[core, m],
            device_id=(4 * peer(o) + 2 * zh + core, r), device_id_type=MESH,
        )

    def s2_pass(o):
        src = source(o)
        return pltpu.make_async_remote_copy(
            src_ref=gathered.at[core, src], dst_ref=gathered.at[core, src],
            send_sem=s2_fwd.at[o], recv_sem=s2_recv.at[core, src],
            device_id=(other, r), device_id_type=MESH,
        )

    def arrival(part, src):
        return pltpu.make_async_copy(gathered.at[part, src], gathered.at[part, src], s2_recv.at[part, src])

    def s2_start(o, c):
        s2_copy(o).start()
        return c

    lax.fori_loop(1, 16, s2_start, 0)
    s2_pass(0).start()

    def hand_on(o, c):
        arrival(core, source(o)).wait()
        s2_pass(o).start()
        return c

    lax.fori_loop(1, 4, hand_on, 0)
    load_vec.wait()

    def chunk_in(q, c):
        @pl.when(q < 3)
        def _():
            lax.fori_loop(4 * q + 4, 4 * q + 8, hand_on, 0)

        xs = (x + 4 - q) % 4

        def wait_sibling(o, c2):
            arrival(1 - core, source(o)).wait()
            return c2

        lax.fori_loop(4 * q, 4 * q + 4, wait_sibling, 0)
        parts = []
        for half in range(2):
            main = jnp.concatenate([gathered[half, 4 * xs + k, 0:80] for k in range(4)], axis=0)
            tail = jnp.concatenate([gathered[half, 4 * xs + k, 80:96] for k in range(4)], axis=0)
            tail = jnp.where(u_match320, dot(tailsel[...], tail), 0.0).astype(BF16)
            parts.append(jnp.concatenate([main, tail], axis=1))
        first = pl.multiple_of(ROW4 * xs, ROW4)
        goal = colg[pl.ds(first, ROW4), :]

        def put(begin, end, value):
            value = jnp.concatenate([value[80 * k : 80 * k + CHIP] for k in range(4)], axis=0)
            width = end - begin
            wide_goal = jnp.concatenate([goal] * (width // 128), axis=1)
            keep = wide_goal == irr_ref[:, begin:end]
            texp[:, begin:end] = jnp.where(keep, value, 0.0).astype(BF16)

        put(0, 512, dot(parts[0], expand[0:256, 0:512]))
        put(512, 768, dot(jnp.concatenate(parts, axis=1), expand[:, 512:768]))
        put(768, 1152, dot(parts[1], expand[256:512, 768:1152]))
        rows_h = vec[pl.ds(pl.multiple_of(HALF * h, HALF), HALF), :]
        inner[pl.ds(first, ROW4), :] = dot_nt(texp[...], rows_h).astype(BF16)
        return c

    lax.fori_loop(0, 4, chunk_in, 0)

    def sib_copy(d):
        return pltpu.make_async_remote_copy(
            src_ref=outgoing.at[d], dst_ref=sibling.at[d // 2],
            send_sem=s3_sib_send.at[d // 2], recv_sem=s3_sib_recv.at[d // 2],
            device_id=(other, r), device_id_type=MESH,
        )

    def s3_copy(d):
        return pltpu.make_async_remote_copy(
            src_ref=summed.at[d // 2], dst_ref=rx3.at[m],
            send_sem=s3_send.at[d // 2], recv_sem=s3_recv.at[m],
            device_id=(4 * d + 2 * zh + core, r), device_id_type=MESH,
        )

    def merge(q):
        xd = (x + q + 1) % 4
        for e in range(2):
            d = 4 * xd + 2 * e + core
            slot = 2 * xd + e
            pltpu.make_async_copy(sibling.at[slot], sibling.at[slot], s3_sib_recv.at[slot]).wait()
            total = (outgoing[d].astype(F32) + sibling[slot].astype(F32)).astype(BF16)

            @pl.when(d == m)
            def _():
                rx3[m] = total

            @pl.when(d != m)
            def _():
                summed[slot] = total
                s3_copy(d).start()

    def chunk_out(q, c):
        xd = (x + q + 1) % 4
        first = pl.multiple_of(ROW4 * xd, ROW4)
        sig = dot(vec[pl.ds(first, ROW4), :], inner[...])
        goal = colg[pl.ds(first, ROW4), :]
        wide_goal = jnp.concatenate([goal] * 4 + [goal[:, :64]], axis=1)
        keep = wide_goal == irrhalf[pl.ds(h, 1), :]
        sig = jnp.where(keep, sig, 0.0).astype(BF16)
        short = dot_nt(sig, reduce_r[...])
        tail = jnp.where(u_match, short[:, 128:], 0.0).astype(BF16)
        tail = dot(tail_pack4, tail)
        for k in range(4):
            block = jnp.concatenate([short[CHIP * k : CHIP * k + CHIP, :128], jnp.zeros((8, 128), F32)], axis=0)
            outgoing[4 * xd + k, 0:80] = block.astype(BF16)
            outgoing[4 * xd + k, 80:96] = tail[16 * k : 16 * k + 16].astype(BF16)
        for e in range(2):
            sib_copy(4 * xd + 2 * e + 1 - core).start()

        @pl.when(q > 0)
        def _():
            merge(q - 1)
        return c

    lax.fori_loop(0, 4, chunk_out, 0)
    merge(3)

    def s4_copy(t):
        return pltpu.make_async_remote_copy(
            src_ref=tx4.at[t], dst_ref=rx4.at[2 * p + zh],
            send_sem=s4_send.at[t], recv_sem=s4_recv,
            device_id=(4 * m + t % 4, 4 * h + t // 4), device_id_type=MESH,
        )

    def s4_is_me(t):
        return jnp.logical_and(t % 4 == 2 * zh + core, 4 * h + t // 4 == r)

    reducer = core == y % 2

    @pl.when(reducer)
    def _():
        def take(o, c):
            src = source(o)
            pltpu.make_async_copy(rx3.at[src], rx3.at[src], s3_recv.at[src]).wait()
            return c

        lax.fori_loop(1, 16, take, 0)
        total = rx3[0].astype(F32)
        for s in range(1, 16):
            total = total + rx3[s].astype(F32)
        high = total.astype(BF16)
        low = (total - high.astype(F32)).astype(BF16)
        result = jnp.zeros((32, 512), F32)
        for piece in (high, low):
            tail = jnp.where(u_match320[:80], dot(tailsel[0:80, 0:16], piece[80:96]), 0.0).astype(BF16)
            full = jnp.concatenate([piece[0:80], tail], axis=1)
            by_row = dot(rowsel_t, full).astype(BF16)
            by_row = jnp.concatenate([by_row[32 * k : 32 * k + 32] for k in range(3)], axis=1)
            result = result + dot_nt(by_row, lanek[...])
        for t in range(16):
            tx4[t] = result[8 * (t % 4) : 8 * (t % 4) + 8, 128 * (t // 4) : 128 * (t // 4) + 128]

        def s4_start(t, c):
            me = s4_is_me(t)

            @pl.when(jnp.logical_not(me))
            def _():
                s4_copy(t).start()

            @pl.when(me)
            def _():
                pltpu.make_async_copy(tx4.at[t], rx4.at[2 * p + zh], s4_recv).start()
            return c

        lax.fori_loop(0, 16, s4_start, 0)

    pltpu.make_async_copy(rx4, rx4, s4_recv).wait()
    got = jnp.concatenate([rx4[2 * q] + rx4[2 * q + 1] for q in range(4)], axis=0).astype(BF16)
    up_row, up_col = iota((CHIP, 32), 0), iota((CHIP, 32), 1)
    up_third = (up_row >= 24).astype(I32) + (up_row >= 48).astype(I32)
    unpick = jnp.logical_and(
        (up_col >> 3) == (up_row & 3), (up_col & 7) == (up_row >> 2) - 6 * up_third
    ).astype(BF16)
    spread_out = jnp.where(lane_group == third, dot(unpick, got), 0.0).astype(BF16)
    final = dot(spread_out, rpack[...]) * own[...]
    for dd in range(TILE):
        out_ref[dd] = final[4 * dd : 4 * dd + 4, :].astype(BF16)

    def s1_done(t, c):
        @pl.when(jnp.logical_not(s1_is_me(t)))
        def _():
            s1_copy(t).wait_send()
        return c

    lax.fori_loop(0, 16, s1_done, 0)
    s2_pass(0).wait_send()

    def s2_done(o, c):
        s2_copy(o).wait_send()
        s2_pass(o).wait_send()
        return c

    lax.fori_loop(1, 16, s2_done, 0)

    def s3_done(n, c):
        sib_copy(2 * n + 1 - core).wait_send()

        @pl.when(2 * n + core != m)
        def _():
            s3_copy(2 * n + core).wait_send()
        return c

    lax.fori_loop(0, 8, s3_done, 0)

    @pl.when(reducer)
    def _():
        def s4_done(t, c):
            @pl.when(jnp.logical_not(s4_is_me(t)))
            def _():
                s4_copy(t).wait_send()
            return c

        lax.fori_loop(0, 16, s4_done, 0)


def per_device(amplitudes, cholesky, virt_irreps, pair_irreps):
    vmem = pl.BlockSpec(memory_space=pltpu.VMEM)
    dma, reg = pltpu.SemaphoreType.DMA, pltpu.SemaphoreType.REGULAR
    return pl.pallas_call(
        kernel,
        out_shape=jax.ShapeDtypeStruct(amplitudes.shape, BF16),
        in_specs=[vmem, pl.BlockSpec(memory_space=pl.ANY), vmem, pl.BlockSpec(memory_space=pltpu.SMEM)],
        out_specs=vmem,
        scratch_shapes=[
            pltpu.VMEM((NV, NV), BF16),
            pltpu.VMEM((8, BLK), I32),
            pltpu.VMEM((8, BLK), I32),
            pltpu.VMEM((8, HALF), I32),
            pltpu.VMEM((1, NV), I32),
            pltpu.VMEM((8, HALF), I32),
            pltpu.VMEM((NV, 128), I32),
            pltpu.VMEM((CHIP, BLK), F32),
            pltpu.VMEM((CHIP, BLK), F32),
            pltpu.VMEM((128, BLK), BF16),
            pltpu.VMEM((512, 768), BF16),
            pltpu.VMEM((512, NV), BF16),
            pltpu.VMEM((256, HALF), BF16),
            pltpu.VMEM((320, 64), BF16),
            pltpu.VMEM((4, 8, 128), F32),
            pltpu.VMEM((16, 8, 128), F32),
            pltpu.VMEM((2, 16, 96, 128), BF16),
            pltpu.VMEM((ROW4, NV), BF16),
            pltpu.VMEM((NV, HALF), BF16),
            pltpu.VMEM((16, 96, 128), BF16),
            pltpu.VMEM((8, 96, 128), BF16),
            pltpu.VMEM((8, 96, 128), BF16),
            pltpu.VMEM((16, 96, 128), BF16),
            pltpu.VMEM((16, 8, 128), F32),
            pltpu.VMEM((8, 8, 128), F32),
            dma,
            dma((16,)), dma,
            dma((16,)), dma((16,)), dma((2, 16)),
            dma((8,)), dma((8,)),
            dma((8,)), dma((16,)),
            dma((16,)), dma,
        ],
        compiler_params=pltpu.CompilerParams(
            collective_id=0, has_side_effects=True, vmem_limit_bytes=40 * 1024 * 1024
        ),
        cost_estimate=pl.CostEstimate(flops=3_060_000_000, bytes_accessed=2_700_000, transcendentals=0),
    )(amplitudes, cholesky, virt_irreps.reshape(1, NV), pair_irreps)


def solution(mesh):
    placed = (P("blk", None, "row"), P("blk", None, None), P(), P())
    return jax.shard_map(
        per_device, mesh=mesh, in_specs=placed, out_specs=P("blk", None, "row"), check_vma=False
    )
```

```python
import jax
import jax.numpy as jnp
from jax import lax
from jax.experimental import pallas as pl
from jax.experimental.pallas import tpu as pltpu
from jax.sharding import PartitionSpec as P

NV = 1152
BLK = 144
TILE = 18
HALF = 576
CHIP = 72
ROW4 = 288
F32 = jnp.float32
BF16 = jnp.bfloat16
I32 = jnp.int32
MESH = pl.DeviceIdType.MESH


def iota(shape, dim):
    return lax.broadcasted_iota(I32, shape, dim)


def dot(a, b):
    return jnp.dot(a, b, preferred_element_type=F32)


def dot_nt(a, b):
    return lax.dot_general(a, b, (((1,), (1,)), ((), ())), preferred_element_type=F32)


def lane_key(lane):
    main = ((lane >> 5) << 6) + (lane & 31)
    tail = (((lane >> 2) & 3) << 6) + 32 + (lane & 3)
    return jnp.where(lane < 128, main, tail)


def over36(v):
    return (v >= 36).astype(I32) + (v >= 72).astype(I32) + (v >= 108).astype(I32)


def kernel(
    amp_hbm, chol_ref, irr_hbm, pair_hbm, out_ref,
    amp_ref, irr9, pair_ref, irr_ref, vec, irrblk, rankblk, irrhalf, rankrow, rankhalf, colg, x32, own, rpack,
    lanek, expand, reduce_r, tailsel, tx1, rx1, gathered, texp, inner, outgoing,
    sibling, summed, rx3, tx4, rx4,
    vec_sem, small_sem, s1_send, s1_recv, s2_send, s2_fwd, s2_recv, s3_sib_send, s3_sib_recv,
    s3_send, s3_recv, s4_send, s4_recv,
):
    j = lax.axis_index("blk")
    r = lax.axis_index("row")
    m, zh, core = j // 4, (j // 2) % 2, j % 2
    x, y = m // 4, m % 4
    p, h = r % 4, 1 - r // 4
    z = 8 * zh + r
    other = 4 * m + 2 * zh + (1 - core)

    load_vec = pltpu.make_async_copy(chol_ref.at[0], vec, vec_sem)
    loads = [
        pltpu.make_async_copy(irr_hbm, irr9, small_sem.at[0]),
        pltpu.make_async_copy(pair_hbm, pair_ref, small_sem.at[1]),
        pltpu.make_async_copy(amp_hbm, amp_ref, small_sem.at[2]),
    ]
    for load in loads:
        load.start()
    load_vec.start()

    barrier = pltpu.get_barrier_semaphore()

    def ring_far(t):
        return 8 + (t // 2) * (1 - 2 * (t % 2)) - t % 2

    def greet_line(t, c):
        zd = (z + ring_far(t)) % 16
        for k in range(2):
            @pl.when(jnp.logical_or(t < 15, core != k))
            def _():
                pl.semaphore_signal(
                    barrier, inc=1, device_id=(4 * m + 2 * (zd // 8) + k, zd % 8), device_id_type=MESH
                )
        return c

    lax.fori_loop(0, 16, greet_line, 0)

    def far(i):
        return 2 + i // 2 - (i % 2) * (1 + 2 * (i // 2))

    def peer(o):
        return 4 * ((x + far(o // 4)) % 4) + (y + far(o % 4)) % 4

    def source(o):
        return 4 * ((x + 4 - far(o // 4)) % 4) + (y + 4 - far(o % 4)) % 4

    def greet_plane(o, c):
        pl.semaphore_signal(barrier, inc=1, device_id=(4 * peer(o) + 2 * zh + core, r), device_id_type=MESH)
        return c

    lax.fori_loop(0, 15, greet_plane, 0)

    for load in loads:
        load.wait()
    irr = jnp.concatenate([irr9[k : k + 1, :] for k in range(9)], axis=1)
    irr_ref[...] = irr
    upper = (iota((BLK, BLK), 0) < iota((BLK, BLK), 1)).astype(BF16)
    eye = iota((BLK, BLK), 0) == iota((BLK, BLK), 1)
    ones = jnp.ones((BLK, 128), BF16)
    pair_own = pair_ref[p]
    members = []
    for b in range(8):
        irr_b = irr[:, BLK * b : BLK * (b + 1)]
        irrblk[b : b + 1, :] = irr_b
        members.append((jnp.broadcast_to(irr_b, (8, BLK)) == iota((8, BLK), 0)).astype(F32))
        diagonal = jnp.where(eye, jnp.broadcast_to(irr_b, (BLK, BLK)), 0).astype(F32).astype(BF16)
        column = dot(diagonal, ones).astype(I32)
        colg[BLK * b : BLK * (b + 1), :] = jnp.bitwise_xor(column, pair_own)
    irrhalf[0:1, :] = irr[:, :HALF]
    irrhalf[1:2, :] = irr[:, HALF:]
    members = jnp.concatenate(members, axis=0)
    before = members * dot(members.astype(BF16), upper)
    for b in range(8):
        rank_b = jnp.sum(before[8 * b : 8 * b + 8], axis=0, keepdims=True).astype(I32)
        rankblk[b : b + 1, :] = rank_b
        keyed = rank_b + 64 * b
        rankrow[:, BLK * b : BLK * (b + 1)] = keyed
    rankhalf[0:1, :] = rankrow[:, :HALF]
    rankhalf[1:2, :] = rankrow[:, HALF:] - 256

    row72 = iota((CHIP, 1), 0)
    own_index = TILE * j + (row72 >> 2)
    own_irr = jnp.sum(
        jnp.where(iota((CHIP, NV), 1) == own_index, jnp.broadcast_to(irr, (CHIP, NV)), 0).astype(F32),
        axis=1, keepdims=True,
    ).astype(I32)
    pairs_col = jnp.zeros((CHIP, 1), I32)
    for q in range(4):
        pairs_col = jnp.where((row72 & 3) == q, pair_ref[q], pairs_col)
    own_goal = jnp.bitwise_xor(own_irr, pairs_col)
    own_mask = (own_goal == irrblk[pl.ds(r, 1), :]).astype(F32)
    own[...] = own_mask
    lane128 = iota((128, BLK), 0)
    slot128 = lane128 - 36 * over36(lane128)
    rpack[...] = jnp.logical_and(lane128 < 108, slot128 == rankblk[pl.ds(r, 1), :]).astype(BF16)
    for dd in range(TILE):
        x32[4 * dd : 4 * dd + 4, :] = amp_ref[dd].astype(F32)
    masked = (x32[...] * own_mask).astype(BF16)
    lane_group = over36(iota((CHIP, 128), 1))
    third = iota((CHIP, 128), 0)
    third = (third >= 24).astype(I32) + (third >= 48).astype(I32)
    spread = jnp.where(lane_group == third, dot_nt(masked, rpack[...]), 0.0).astype(BF16)
    pk_row, pk_col = iota((32, CHIP), 0), iota((32, CHIP), 1)
    col_third = (pk_col >= 24).astype(I32) + (pk_col >= 48).astype(I32)
    pick = jnp.logical_and(
        (pk_row >> 3) == (pk_col & 3), (pk_row & 7) == (pk_col >> 2) - 6 * col_third
    ).astype(BF16)
    packed = dot(pick, spread)
    for q in range(4):
        tx1[q] = packed[8 * q : 8 * q + 8]

    pl.semaphore_wait(barrier, 46)

    slot_me = (r % 4) * 4 + 2 * zh + core

    def s1_copy(t):
        zd = (z + ring_far(t)) % 16
        return pltpu.make_async_remote_copy(
            src_ref=tx1.at[zd % 4], dst_ref=rx1.at[slot_me],
            send_sem=s1_send.at[t], recv_sem=s1_recv,
            device_id=(4 * m + 2 * (zd // 8) + r // 4, zd % 8), device_id_type=MESH,
        )

    def s1_is_me(t):
        return jnp.logical_and(core == r // 4, t == 15)

    def s1_start(t, c):
        me = s1_is_me(t)

        @pl.when(jnp.logical_not(me))
        def _():
            s1_copy(t).start()

        @pl.when(me)
        def _():
            pltpu.make_async_copy(tx1.at[p], rx1.at[slot_me], s1_recv).start()
        return c

    lax.fori_loop(0, 16, s1_start, 0)

    col = iota((1, 768), 1)
    key = lane_key(col & 255)
    target = (key >> 6) * 128 + 36 * (col >> 8) + (key & 63)
    lanek[...] = (iota((512, 768), 0) == target).astype(BF16)
    lane_col = iota((512, 1), 0)
    expand[...] = (lane_key(lane_col & 255) + 256 * (lane_col >> 8) == rankrow[...]).astype(BF16)
    reduce_r[...] = (lane_key(iota((256, 1), 0)) == rankhalf[pl.ds(h, 1), :]).astype(BF16)
    ts_row, ts_col = iota((320, 64), 0), iota((320, 64), 1)
    tailsel[...] = jnp.logical_and(
        (ts_row >> 3) == 10 * (ts_col >> 4) + (ts_col & 15), (ts_col & 15) < 10
    ).astype(BF16)
    u_row, u_lane = iota((ROW4, 128), 0), iota((ROW4, 128), 1)
    u_match = (u_row & 7) == (u_lane >> 4)
    u_match320 = (iota((320, 128), 0) & 7) == (iota((320, 128), 1) >> 4)

    def row_target(c):
        return TILE * ((c >> 3) & 3) + 6 * (c >> 5) + (c & 7)

    rs_row, rs_col = iota((80, 96), 0), iota((80, 96), 1)
    rowsel = jnp.logical_and(rs_row == row_target(rs_col), (rs_col & 7) < 6).astype(BF16)
    rt_row, rt_col = iota((96, 80), 0), iota((96, 80), 1)
    rowsel_t = jnp.logical_and(rt_col == row_target(rt_row), (rt_row & 7) < 6).astype(BF16)
    tail_pack = ((iota((16, 80), 1) >> 3) == iota((16, 80), 0)).astype(BF16)
    tp_row, tp_col = iota((64, ROW4), 0), iota((64, ROW4), 1)
    tail_pack4 = jnp.logical_and(
        (tp_col >> 3) == 9 * (tp_row >> 4) + (tp_row & 15), (tp_row & 15) < 9
    ).astype(BF16)

    pltpu.make_async_copy(rx1, rx1, s1_recv).wait()
    arrived = jnp.concatenate([rx1[s] for s in range(16)], axis=0)
    wide = jnp.concatenate([arrived[32 * g : 32 * g + 32] for g in range(4)], axis=1).astype(BF16)
    placed = dot(wide, lanek[...]).astype(BF16)
    stacked = jnp.concatenate([placed[:, 256 * k : 256 * k + 256] for k in range(3)], axis=0)
    rows = dot(rowsel, stacked)
    gathered[core, m, 0:80] = rows[:, :128].astype(BF16)
    tails = jnp.where(u_match320[:80], rows[:, 128:], 0.0).astype(BF16)
    gathered[core, m, 80:96] = dot(tail_pack, tails).astype(BF16)

    def s2_copy(o):
        return pltpu.make_async_remote_copy(
            src_ref=gathered.at[core, m], dst_ref=gathered.at[core, m],
            send_sem=s2_send.at[o], recv_sem=s2_recv.at[core, m],
            device_id=(4 * peer(o) + 2 * zh + core, r), device_id_type=MESH,
        )

    def s2_pass(o):
        src = source(o)
        return pltpu.make_async_remote_copy(
            src_ref=gathered.at[core, src], dst_ref=gathered.at[core, src],
            send_sem=s2_fwd.at[o], recv_sem=s2_recv.at[core, src],
            device_id=(other, r), device_id_type=MESH,
        )

    def arrival(part, src):
        return pltpu.make_async_copy(gathered.at[part, src], gathered.at[part, src], s2_recv.at[part, src])

    def s2_start(o, c):
        s2_copy(o).start()
        return c

    lax.fori_loop(0, 15, s2_start, 0)
    s2_pass(15).start()

    def hand_on(o, c):
        arrival(core, source(o)).wait()
        s2_pass(o).start()
        return c

    lax.fori_loop(0, 4, hand_on, 0)
    load_vec.wait()

    def chunk_in(q, c):
        @pl.when(q < 3)
        def _():
            lax.fori_loop(4 * q + 4, 4 * q + 8 - q // 2, hand_on, 0)

        xs = (x + 4 - far(q)) % 4

        def wait_sibling(o, c2):
            arrival(1 - core, source(o)).wait()
            return c2

        lax.fori_loop(4 * q, 4 * q + 4, wait_sibling, 0)
        parts = []
        for half in range(2):
            main = jnp.concatenate([gathered[half, 4 * xs + k, 0:80] for k in range(4)], axis=0)
            tail = jnp.concatenate([gathered[half, 4 * xs + k, 80:96] for k in range(4)], axis=0)
            tail = jnp.where(u_match320, dot(tailsel[...], tail), 0.0).astype(BF16)
            parts.append(jnp.concatenate([main, tail], axis=1))
        first = pl.multiple_of(ROW4 * xs, ROW4)
        goal = colg[pl.ds(first, ROW4), :]

        def put(begin, end, value):
            value = jnp.concatenate([value[80 * k : 80 * k + CHIP] for k in range(4)], axis=0)
            width = end - begin
            wide_goal = jnp.concatenate([goal] * (width // 128), axis=1)
            keep = wide_goal == irr_ref[:, begin:end]
            texp[:, begin:end] = jnp.where(keep, value, 0.0).astype(BF16)

        put(0, 512, dot(parts[0], expand[0:256, 0:512]))
        put(512, 768, dot(jnp.concatenate(parts, axis=1), expand[:, 512:768]))
        put(768, 1152, dot(parts[1], expand[256:512, 768:1152]))
        rows_h = vec[pl.ds(pl.multiple_of(HALF * h, HALF), HALF), :]
        inner[pl.ds(first, ROW4), :] = dot_nt(texp[...], rows_h).astype(BF16)
        return c

    lax.fori_loop(0, 4, chunk_in, 0)

    def sib_copy(d):
        return pltpu.make_async_remote_copy(
            src_ref=outgoing.at[d], dst_ref=sibling.at[d // 2],
            send_sem=s3_sib_send.at[d // 2], recv_sem=s3_sib_recv.at[d // 2],
            device_id=(other, r), device_id_type=MESH,
        )

    def s3_copy(d):
        return pltpu.make_async_remote_copy(
            src_ref=summed.at[d // 2], dst_ref=rx3.at[m],
            send_sem=s3_send.at[d // 2], recv_sem=s3_recv.at[m],
            device_id=(4 * d + 2 * zh + core, r), device_id_type=MESH,
        )

    def merge(q):
        xd = (x + far(q)) % 4
        for e in range(2):
            d = 4 * xd + 2 * e + core
            slot = 2 * xd + e
            pltpu.make_async_copy(sibling.at[slot], sibling.at[slot], s3_sib_recv.at[slot]).wait()
            total = (outgoing[d].astype(F32) + sibling[slot].astype(F32)).astype(BF16)

            @pl.when(d == m)
            def _():
                rx3[m] = total

            @pl.when(d != m)
            def _():
                summed[slot] = total
                s3_copy(d).start()

    def chunk_out(q, c):
        xd = (x + far(q)) % 4
        first = pl.multiple_of(ROW4 * xd, ROW4)
        sig = dot(vec[pl.ds(first, ROW4), :], inner[...])
        goal = colg[pl.ds(first, ROW4), :]
        wide_goal = jnp.concatenate([goal] * 4 + [goal[:, :64]], axis=1)
        keep = wide_goal == irrhalf[pl.ds(h, 1), :]
        sig = jnp.where(keep, sig, 0.0).astype(BF16)
        short = dot_nt(sig, reduce_r[...])
        tail = jnp.where(u_match, short[:, 128:], 0.0).astype(BF16)
        tail = dot(tail_pack4, tail)
        for k in range(4):
            block = jnp.concatenate([short[CHIP * k : CHIP * k + CHIP, :128], jnp.zeros((8, 128), F32)], axis=0)
            outgoing[4 * xd + k, 0:80] = block.astype(BF16)
            outgoing[4 * xd + k, 80:96] = tail[16 * k : 16 * k + 16].astype(BF16)
        for e in range(2):
            sib_copy(4 * xd + 2 * e + 1 - core).start()

        @pl.when(q > 0)
        def _():
            merge(q - 1)
        return c

    lax.fori_loop(0, 4, chunk_out, 0)
    merge(3)

    def s4_copy(t):
        rr, tile = t // 4, t % 4
        return pltpu.make_async_remote_copy(
            src_ref=tx4.at[t], dst_ref=rx4.at[2 * p + zh],
            send_sem=s4_send.at[t], recv_sem=s4_recv,
            device_id=(4 * m + tile, 4 * h + rr), device_id_type=MESH,
        )

    reducer = core == y % 2

    @pl.when(reducer)
    def _():
        def take(o, c):
            src = source(o)
            pltpu.make_async_copy(rx3.at[src], rx3.at[src], s3_recv.at[src]).wait()
            return c

        lax.fori_loop(0, 15, take, 0)
        total = rx3[0].astype(F32)
        for s in range(1, 16):
            total = total + rx3[s].astype(F32)
        total = total.astype(BF16)
        tail = jnp.where(u_match320[:80], dot(tailsel[0:80, 0:16], total[80:96]), 0.0).astype(BF16)
        by_row = dot(rowsel_t, jnp.concatenate([total[0:80], tail], axis=1)).astype(BF16)
        by_row = jnp.concatenate([by_row[32 * k : 32 * k + 32] for k in range(3)], axis=1)
        result = dot_nt(by_row, lanek[...])
        for t in range(16):
            tx4[t] = result[8 * (t % 4) : 8 * (t % 4) + 8, 128 * (t // 4) : 128 * (t // 4) + 128]

        def s4_start(t, c):
            zd = (z + ring_far(t)) % 16

            @pl.when((zd % 8) // 4 == h)
            def _():
                for k in range(2):
                    s4_copy(4 * (zd % 4) + 2 * (zd // 8) + k).start()
            return c

        lax.fori_loop(0, 16, s4_start, 0)

    def s1_done(t, c):
        @pl.when(jnp.logical_not(s1_is_me(t)))
        def _():
            s1_copy(t).wait_send()
        return c

    lax.fori_loop(0, 16, s1_done, 0)
    s2_pass(15).wait_send()

    def s2_done(o, c):
        s2_copy(o).wait_send()
        s2_pass(o).wait_send()
        return c

    lax.fori_loop(0, 15, s2_done, 0)

    def s3_done(n, c):
        sib_copy(2 * n + 1 - core).wait_send()

        @pl.when(2 * n + core != m)
        def _():
            s3_copy(2 * n + core).wait_send()
        return c

    lax.fori_loop(0, 8, s3_done, 0)

    @pl.when(reducer)
    def _():
        def s4_done(t, c):
            s4_copy(t).wait_send()
            return c

        lax.fori_loop(0, 16, s4_done, 0)

    pltpu.make_async_copy(rx4, rx4, s4_recv).wait()
    got = jnp.concatenate([rx4[2 * q] + rx4[2 * q + 1] for q in range(4)], axis=0).astype(BF16)
    up_row, up_col = iota((CHIP, 32), 0), iota((CHIP, 32), 1)
    up_third = (up_row >= 24).astype(I32) + (up_row >= 48).astype(I32)
    unpick = jnp.logical_and(
        (up_col >> 3) == (up_row & 3), (up_col & 7) == (up_row >> 2) - 6 * up_third
    ).astype(BF16)
    spread_out = jnp.where(lane_group == third, dot(unpick, got), 0.0).astype(BF16)
    final = dot(spread_out, rpack[...]) * own[...]
    for dd in range(TILE):
        out_ref[dd] = final[4 * dd : 4 * dd + 4, :].astype(BF16)


def per_device(amplitudes, cholesky, virt_irreps, pair_irreps):
    vmem = pl.BlockSpec(memory_space=pltpu.VMEM)
    dma = pltpu.SemaphoreType.DMA
    return pl.pallas_call(
        kernel,
        out_shape=jax.ShapeDtypeStruct(amplitudes.shape, BF16),
        in_specs=[pl.BlockSpec(memory_space=pltpu.HBM)] * 4,
        out_specs=vmem,
        scratch_shapes=[
            pltpu.VMEM((TILE, 4, BLK), BF16),
            pltpu.VMEM((9, 128), I32),
            pltpu.SMEM((4,), I32),
            pltpu.VMEM((1, NV), I32),
            pltpu.VMEM((NV, NV), BF16),
            pltpu.VMEM((8, BLK), I32),
            pltpu.VMEM((8, BLK), I32),
            pltpu.VMEM((8, HALF), I32),
            pltpu.VMEM((1, NV), I32),
            pltpu.VMEM((8, HALF), I32),
            pltpu.VMEM((NV, 128), I32),
            pltpu.VMEM((CHIP, BLK), F32),
            pltpu.VMEM((CHIP, BLK), F32),
            pltpu.VMEM((128, BLK), BF16),
            pltpu.VMEM((512, 768), BF16),
            pltpu.VMEM((512, NV), BF16),
            pltpu.VMEM((256, HALF), BF16),
            pltpu.VMEM((320, 64), BF16),
            pltpu.VMEM((4, 8, 128), F32),
            pltpu.VMEM((16, 8, 128), F32),
            pltpu.VMEM((2, 16, 96, 128), BF16),
            pltpu.VMEM((ROW4, NV), BF16),
            pltpu.VMEM((NV, HALF), BF16),
            pltpu.VMEM((16, 96, 128), BF16),
            pltpu.VMEM((8, 96, 128), BF16),
            pltpu.VMEM((8, 96, 128), BF16),
            pltpu.VMEM((16, 96, 128), BF16),
            pltpu.VMEM((16, 8, 128), F32),
            pltpu.VMEM((8, 8, 128), F32),
            dma, dma((3,)),
            dma((16,)), dma,
            dma((16,)), dma((16,)), dma((2, 16)),
            dma((8,)), dma((8,)),
            dma((8,)), dma((16,)),
            dma((16,)), dma,
        ],
        compiler_params=pltpu.CompilerParams(
            collective_id=0, has_side_effects=True, vmem_limit_bytes=62 * 1024 * 1024
        ),
        cost_estimate=pl.CostEstimate(flops=3_060_000_000, bytes_accessed=2_700_000, transcendentals=0),
    )(amplitudes, cholesky, virt_irreps.reshape(9, 128), pair_irreps)


def solution(mesh):
    placed = (P("blk", None, "row"), P("blk", None, None), P(), P())
    return jax.shard_map(
        per_device, mesh=mesh, in_specs=placed, out_specs=P("blk", None, "row"), check_vma=False
    )
```

```python
import jax
import jax.numpy as jnp
from jax import lax
from jax.experimental import pallas as pl
from jax.experimental.pallas import tpu as pltpu
from jax.sharding import PartitionSpec as P

NV = 1152
BLK = 144
TILE = 18
HALF = 576
CHIP = 72
ROW4 = 288
F32 = jnp.float32
BF16 = jnp.bfloat16
I32 = jnp.int32
MESH = pl.DeviceIdType.MESH


def iota(shape, dim):
    return lax.broadcasted_iota(I32, shape, dim)


def dot(a, b):
    return jnp.dot(a, b, preferred_element_type=F32)


def dot_nt(a, b):
    return lax.dot_general(a, b, (((1,), (1,)), ((), ())), preferred_element_type=F32)


def lane_key(lane):
    main = ((lane >> 5) << 6) + (lane & 31)
    tail = (((lane >> 2) & 3) << 6) + 32 + (lane & 3)
    return jnp.where(lane < 128, main, tail)


def over36(v):
    return (v >= 36).astype(I32) + (v >= 72).astype(I32) + (v >= 108).astype(I32)


def kernel(
    amp_hbm, chol_ref, irr_hbm, pair_hbm, out_ref,
    amp_ref, irr9, pair_ref, irr_ref, vec, irrblk, rankblk, irrhalf, rankrow, rankhalf, colg, x32, own, rpack,
    lanek, expand, reduce_r, tailsel, tx1, rx1, gathered, texp, inner, outgoing,
    sibling, summed, rx3, tx4, rx4,
    vec_sem, small_sem, s1_send, s1_recv, s2_send, s2_fwd, s2_recv, s3_sib_send, s3_sib_recv,
    s3_send, s3_recv, s4_send, s4_recv,
):
    j = lax.axis_index("blk")
    r = lax.axis_index("row")
    m, zh, core = j // 4, (j // 2) % 2, j % 2
    x, y = m // 4, m % 4
    p, h = r % 4, 1 - r // 4
    z = 8 * zh + r
    other = 4 * m + 2 * zh + (1 - core)

    load_vec = pltpu.make_async_copy(chol_ref.at[0], vec, vec_sem)
    loads = [
        pltpu.make_async_copy(irr_hbm, irr9, small_sem.at[0]),
        pltpu.make_async_copy(pair_hbm, pair_ref, small_sem.at[1]),
        pltpu.make_async_copy(amp_hbm, amp_ref, small_sem.at[2]),
    ]
    for load in loads:
        load.start()
    load_vec.start()

    barrier = pltpu.get_barrier_semaphore()

    def ring_far(t):
        return 8 + (t // 2) * (1 - 2 * (t % 2)) - t % 2

    def greet_line(t, c):
        zd = (z + ring_far(t)) % 16
        for k in range(2):
            @pl.when(jnp.logical_or(t < 15, core != k))
            def _():
                pl.semaphore_signal(
                    barrier, inc=1, device_id=(4 * m + 2 * (zd // 8) + k, zd % 8), device_id_type=MESH
                )
        return c

    lax.fori_loop(0, 16, greet_line, 0)

    def far(i):
        return 2 + i // 2 - (i % 2) * (1 + 2 * (i // 2))

    def peer(o):
        return 4 * ((x + far(o % 4)) % 4) + (y + far(o // 4)) % 4

    def source(o):
        return 4 * ((x + 4 - far(o % 4)) % 4) + (y + 4 - far(o // 4)) % 4

    def greet_plane(o, c):
        pl.semaphore_signal(barrier, inc=1, device_id=(4 * peer(o) + 2 * zh + core, r), device_id_type=MESH)
        return c

    lax.fori_loop(0, 15, greet_plane, 0)

    for load in loads:
        load.wait()
    irr = jnp.concatenate([irr9[k : k + 1, :] for k in range(9)], axis=1)
    irr_ref[...] = irr
    upper = (iota((BLK, BLK), 0) < iota((BLK, BLK), 1)).astype(BF16)
    eye = iota((BLK, BLK), 0) == iota((BLK, BLK), 1)
    ones = jnp.ones((BLK, 128), BF16)
    pair_own = pair_ref[p]
    members = []
    for b in range(8):
        irr_b = irr[:, BLK * b : BLK * (b + 1)]
        irrblk[b : b + 1, :] = irr_b
        members.append((jnp.broadcast_to(irr_b, (8, BLK)) == iota((8, BLK), 0)).astype(F32))
        diagonal = jnp.where(eye, jnp.broadcast_to(irr_b, (BLK, BLK)), 0).astype(F32).astype(BF16)
        column = dot(diagonal, ones).astype(I32)
        colg[BLK * b : BLK * (b + 1), :] = jnp.bitwise_xor(column, pair_own)
    irrhalf[0:1, :] = irr[:, :HALF]
    irrhalf[1:2, :] = irr[:, HALF:]
    members = jnp.concatenate(members, axis=0)
    before = members * dot(members.astype(BF16), upper)
    for b in range(8):
        rank_b = jnp.sum(before[8 * b : 8 * b + 8], axis=0, keepdims=True).astype(I32)
        rankblk[b : b + 1, :] = rank_b
        keyed = rank_b + 64 * b
        rankrow[:, BLK * b : BLK * (b + 1)] = keyed
    rankhalf[0:1, :] = rankrow[:, :HALF]
    rankhalf[1:2, :] = rankrow[:, HALF:] - 256

    row72 = iota((CHIP, 1), 0)
    own_index = TILE * j + (row72 >> 2)
    own_irr = jnp.sum(
        jnp.where(iota((CHIP, NV), 1) == own_index, jnp.broadcast_to(irr, (CHIP, NV)), 0).astype(F32),
        axis=1, keepdims=True,
    ).astype(I32)
    pairs_col = jnp.zeros((CHIP, 1), I32)
    for q in range(4):
        pairs_col = jnp.where((row72 & 3) == q, pair_ref[q], pairs_col)
    own_goal = jnp.bitwise_xor(own_irr, pairs_col)
    own_mask = (own_goal == irrblk[pl.ds(r, 1), :]).astype(F32)
    own[...] = own_mask
    lane128 = iota((128, BLK), 0)
    slot128 = lane128 - 36 * over36(lane128)
    rpack[...] = jnp.logical_and(lane128 < 108, slot128 == rankblk[pl.ds(r, 1), :]).astype(BF16)
    for dd in range(TILE):
        x32[4 * dd : 4 * dd + 4, :] = amp_ref[dd].astype(F32)
    masked = (x32[...] * own_mask).astype(BF16)
    lane_group = over36(iota((CHIP, 128), 1))
    third = iota((CHIP, 128), 0)
    third = (third >= 24).astype(I32) + (third >= 48).astype(I32)
    spread = jnp.where(lane_group == third, dot_nt(masked, rpack[...]), 0.0).astype(BF16)
    pk_row, pk_col = iota((32, CHIP), 0), iota((32, CHIP), 1)
    col_third = (pk_col >= 24).astype(I32) + (pk_col >= 48).astype(I32)
    pick = jnp.logical_and(
        (pk_row >> 3) == (pk_col & 3), (pk_row & 7) == (pk_col >> 2) - 6 * col_third
    ).astype(BF16)
    packed = dot(pick, spread)
    for q in range(4):
        tx1[q] = packed[8 * q : 8 * q + 8]

    pl.semaphore_wait(barrier, 46)

    slot_me = (r % 4) * 4 + 2 * zh + core

    def s1_copy(t):
        zd = (z + ring_far(t)) % 16
        return pltpu.make_async_remote_copy(
            src_ref=tx1.at[zd % 4], dst_ref=rx1.at[slot_me],
            send_sem=s1_send.at[t], recv_sem=s1_recv,
            device_id=(4 * m + 2 * (zd // 8) + r // 4, zd % 8), device_id_type=MESH,
        )

    def s1_is_me(t):
        return jnp.logical_and(core == r // 4, t == 15)

    def s1_start(t, c):
        if t < 15:
            s1_copy(t).start()
            return c
        me = core == r // 4

        @pl.when(jnp.logical_not(me))
        def _():
            s1_copy(t).start()

        @pl.when(me)
        def _():
            pltpu.make_async_copy(tx1.at[p], rx1.at[slot_me], s1_recv).start()
        return c

    for t in range(16):
        s1_start(t, 0)

    col = iota((1, 768), 1)
    key = lane_key(col & 255)
    target = (key >> 6) * 128 + 36 * (col >> 8) + (key & 63)
    lanek[...] = (iota((512, 768), 0) == target).astype(BF16)
    lane_col = iota((512, 1), 0)
    expand[...] = (lane_key(lane_col & 255) + 256 * (lane_col >> 8) == rankrow[...]).astype(BF16)
    reduce_r[...] = (lane_key(iota((256, 1), 0)) == rankhalf[pl.ds(h, 1), :]).astype(BF16)
    ts_row, ts_col = iota((320, 64), 0), iota((320, 64), 1)
    tailsel[...] = jnp.logical_and(
        (ts_row >> 3) == 10 * (ts_col >> 4) + (ts_col & 15), (ts_col & 15) < 10
    ).astype(BF16)
    u_row, u_lane = iota((ROW4, 128), 0), iota((ROW4, 128), 1)
    u_match = (u_row & 7) == (u_lane >> 4)
    u_match320 = (iota((320, 128), 0) & 7) == (iota((320, 128), 1) >> 4)

    def row_target(c):
        return TILE * ((c >> 3) & 3) + 6 * (c >> 5) + (c & 7)

    rs_row, rs_col = iota((80, 96), 0), iota((80, 96), 1)
    rowsel = jnp.logical_and(rs_row == row_target(rs_col), (rs_col & 7) < 6).astype(BF16)
    rt_row, rt_col = iota((96, 80), 0), iota((96, 80), 1)
    rowsel_t = jnp.logical_and(rt_col == row_target(rt_row), (rt_row & 7) < 6).astype(BF16)
    rq_row, rq_col = iota((96, 16), 0), iota((96, 16), 1)
    rowsel_tail = jnp.logical_and(rq_col == row_target(rq_row) >> 3, (rq_row & 7) < 6).astype(BF16)
    row_u = (row_target(iota((96, 128), 0)) & 7) == (iota((96, 128), 1) >> 4)
    tail_pack = ((iota((16, 80), 1) >> 3) == iota((16, 80), 0)).astype(BF16)
    tp_row, tp_col = iota((64, ROW4), 0), iota((64, ROW4), 1)
    tail_pack4 = jnp.logical_and(
        (tp_col >> 3) == 9 * (tp_row >> 4) + (tp_row & 15), (tp_row & 15) < 9
    ).astype(BF16)

    pltpu.make_async_copy(rx1, rx1, s1_recv).wait()
    arrived = jnp.concatenate([rx1[s] for s in range(16)], axis=0)
    wide = jnp.concatenate([arrived[32 * g : 32 * g + 32] for g in range(4)], axis=1).astype(BF16)
    placed = dot(wide, lanek[...]).astype(BF16)
    stacked = jnp.concatenate([placed[:, 256 * k : 256 * k + 256] for k in range(3)], axis=0)
    rows = dot(rowsel, stacked)
    gathered[core, m, 0:80] = rows[:, :128].astype(BF16)
    tails = jnp.where(u_match320[:80], rows[:, 128:], 0.0).astype(BF16)
    gathered[core, m, 80:96] = dot(tail_pack, tails).astype(BF16)

    def s2_copy(o):
        return pltpu.make_async_remote_copy(
            src_ref=gathered.at[core, m], dst_ref=gathered.at[core, m],
            send_sem=s2_send.at[o], recv_sem=s2_recv.at[core, m],
            device_id=(4 * peer(o) + 2 * zh + core, r), device_id_type=MESH,
        )

    def s2_pass(o):
        src = source(o)
        return pltpu.make_async_remote_copy(
            src_ref=gathered.at[core, src], dst_ref=gathered.at[core, src],
            send_sem=s2_fwd.at[o], recv_sem=s2_recv.at[core, src],
            device_id=(other, r), device_id_type=MESH,
        )

    def arrival(part, src):
        return pltpu.make_async_copy(gathered.at[part, src], gathered.at[part, src], s2_recv.at[part, src])

    def s2_start(o, c):
        s2_copy(o).start()
        return c

    for o in range(15):
        s2_start(o, 0)
    s2_pass(15).start()

    def hand_on(o, c):
        arrival(core, source(o)).wait()
        s2_pass(o).start()
        return c

    lax.fori_loop(0, 15, hand_on, 0)
    load_vec.wait()

    def wait_sibling(o, c):
        arrival(1 - core, source(o)).wait()
        return c

    lax.fori_loop(0, 16, wait_sibling, 0)

    u_all = (iota((1280, 128), 0) & 7) == (iota((1280, 128), 1) >> 4)
    parts = []
    for half in range(2):
        main = jnp.concatenate([gathered[half, chip, 0:80] for chip in range(16)], axis=0)
        tail = jnp.concatenate([
            dot(tailsel[...], jnp.concatenate([gathered[half, 4 * g + k, 80:96] for k in range(4)], axis=0))
            for g in range(4)
        ], axis=0)
        tail = jnp.where(u_all, tail, 0.0).astype(BF16)
        parts.append(jnp.concatenate([main, tail], axis=1))

    def put(begin, end, value):
        value = jnp.concatenate([value[80 * k : 80 * k + CHIP] for k in range(16)], axis=0)
        wide_goal = jnp.concatenate([colg[...]] * ((end - begin) // 128), axis=1)
        keep = wide_goal == irr_ref[:, begin:end]
        texp[:, begin:end] = jnp.where(keep, value, 0.0).astype(BF16)

    put(0, 512, dot(parts[0], expand[0:256, 0:512]))
    put(512, 768, dot(jnp.concatenate(parts, axis=1), expand[:, 512:768]))
    put(768, 1152, dot(parts[1], expand[256:512, 768:1152]))
    rows_h = vec[pl.ds(pl.multiple_of(HALF * h, HALF), HALF), :]
    inner[...] = dot_nt(texp[...], rows_h).astype(BF16)

    def sib_copy(d):
        return pltpu.make_async_remote_copy(
            src_ref=outgoing.at[d], dst_ref=sibling.at[d // 2],
            send_sem=s3_sib_send.at[d // 2], recv_sem=s3_sib_recv.at[d // 2],
            device_id=(other, r), device_id_type=MESH,
        )

    def s3_copy(d):
        return pltpu.make_async_remote_copy(
            src_ref=summed.at[d // 2], dst_ref=rx3.at[m],
            send_sem=s3_send.at[d // 2], recv_sem=s3_recv,
            device_id=(4 * d + 2 * zh + core, r), device_id_type=MESH,
        )

    def merge(q):
        xd = (x + far(q)) % 4
        for e in range(2):
            d = 4 * xd + 2 * e + core
            slot = 2 * xd + e
            pltpu.make_async_copy(sibling.at[slot], sibling.at[slot], s3_sib_recv.at[slot]).wait()
            total = (outgoing[d].astype(F32) + sibling[slot].astype(F32)).astype(BF16)

            @pl.when(d == m)
            def _():
                rx3[m] = total

            @pl.when(d != m)
            def _():
                summed[slot] = total
                s3_copy(d).start()

    def chunk_out(q):
        xd = (x + far(q)) % 4
        first = pl.multiple_of(ROW4 * xd, ROW4)
        sig = dot(vec[pl.ds(first, ROW4), :], inner[...])
        goal = colg[pl.ds(first, ROW4), :]
        wide_goal = jnp.concatenate([goal] * 4 + [goal[:, :64]], axis=1)
        keep = wide_goal == irrhalf[pl.ds(h, 1), :]
        sig = jnp.where(keep, sig, 0.0).astype(BF16)
        short = dot_nt(sig, reduce_r[...])
        tail = jnp.where(u_match, short[:, 128:], 0.0).astype(BF16)
        tail = dot(tail_pack4, tail)
        for k in range(4):
            block = jnp.concatenate([short[CHIP * k : CHIP * k + CHIP, :128], jnp.zeros((8, 128), F32)], axis=0)
            outgoing[4 * xd + k, 0:80] = block.astype(BF16)
            outgoing[4 * xd + k, 80:96] = tail[16 * k : 16 * k + 16].astype(BF16)
        for e in range(2):
            sib_copy(4 * xd + 2 * e + 1 - core).start()

        if q:
            merge(q - 1)

    for q in range(4):
        chunk_out(q)
    merge(3)

    def s4_copy(t):
        rr, tile = t // 4, t % 4
        return pltpu.make_async_remote_copy(
            src_ref=tx4.at[t], dst_ref=rx4.at[2 * p + zh],
            send_sem=s4_send.at[t], recv_sem=s4_recv,
            device_id=(4 * m + tile, 4 * h + rr), device_id_type=MESH,
        )

    reducer = core == y % 2

    @pl.when(reducer)
    def _():
        pltpu.make_async_copy(rx3.at[0:15], rx3.at[0:15], s3_recv).wait()
        total = rx3[0].astype(F32)
        for s in range(1, 16):
            total = total + rx3[s].astype(F32)
        total = total.astype(BF16)
        tail = jnp.where(row_u, dot(rowsel_tail, total[80:96]), 0.0).astype(BF16)
        by_row = jnp.concatenate([dot(rowsel_t, total[0:80]).astype(BF16), tail], axis=1)
        by_row = jnp.concatenate([by_row[32 * k : 32 * k + 32] for k in range(3)], axis=1)
        result = dot_nt(by_row, lanek[...])
        for t in range(16):
            tx4[t] = result[8 * (t % 4) : 8 * (t % 4) + 8, 128 * (t // 4) : 128 * (t // 4) + 128]

        def s4_start(t, c):
            zd = (z + ring_far(t)) % 16

            @pl.when((zd % 8) // 4 == h)
            def _():
                for k in range(2):
                    s4_copy(4 * (zd % 4) + 2 * (zd // 8) + k).start()
            return c

        for t in range(16):
            s4_start(t, 0)

    def s1_done(t, c):
        @pl.when(jnp.logical_not(s1_is_me(t)))
        def _():
            s1_copy(t).wait_send()
        return c

    lax.fori_loop(0, 16, s1_done, 0)
    s2_pass(15).wait_send()

    def s2_done(o, c):
        s2_copy(o).wait_send()
        s2_pass(o).wait_send()
        return c

    lax.fori_loop(0, 15, s2_done, 0)

    def s3_done(n, c):
        sib_copy(2 * n + 1 - core).wait_send()

        @pl.when(2 * n + core != m)
        def _():
            s3_copy(2 * n + core).wait_send()
        return c

    lax.fori_loop(0, 8, s3_done, 0)

    @pl.when(reducer)
    def _():
        def s4_done(t, c):
            s4_copy(t).wait_send()
            return c

        lax.fori_loop(0, 16, s4_done, 0)

    pltpu.make_async_copy(rx4, rx4, s4_recv).wait()
    got = jnp.concatenate([rx4[2 * q] + rx4[2 * q + 1] for q in range(4)], axis=0).astype(BF16)
    up_row, up_col = iota((CHIP, 32), 0), iota((CHIP, 32), 1)
    up_third = (up_row >= 24).astype(I32) + (up_row >= 48).astype(I32)
    unpick = jnp.logical_and(
        (up_col >> 3) == (up_row & 3), (up_col & 7) == (up_row >> 2) - 6 * up_third
    ).astype(BF16)
    spread_out = jnp.where(lane_group == third, dot(unpick, got), 0.0).astype(BF16)
    final = dot(spread_out, rpack[...]) * own[...]
    for dd in range(TILE):
        out_ref[dd] = final[4 * dd : 4 * dd + 4, :].astype(BF16)


def per_device(amplitudes, cholesky, virt_irreps, pair_irreps):
    vmem = pl.BlockSpec(memory_space=pltpu.VMEM)
    dma = pltpu.SemaphoreType.DMA
    return pl.pallas_call(
        kernel,
        out_shape=jax.ShapeDtypeStruct(amplitudes.shape, BF16),
        in_specs=[pl.BlockSpec(memory_space=pltpu.HBM)] * 4,
        out_specs=vmem,
        scratch_shapes=[
            pltpu.VMEM((TILE, 4, BLK), BF16),
            pltpu.VMEM((9, 128), I32),
            pltpu.SMEM((4,), I32),
            pltpu.VMEM((1, NV), I32),
            pltpu.VMEM((NV, NV), BF16),
            pltpu.VMEM((8, BLK), I32),
            pltpu.VMEM((8, BLK), I32),
            pltpu.VMEM((8, HALF), I32),
            pltpu.VMEM((1, NV), I32),
            pltpu.VMEM((8, HALF), I32),
            pltpu.VMEM((NV, 128), I32),
            pltpu.VMEM((CHIP, BLK), F32),
            pltpu.VMEM((CHIP, BLK), F32),
            pltpu.VMEM((128, BLK), BF16),
            pltpu.VMEM((512, 768), BF16),
            pltpu.VMEM((512, NV), BF16),
            pltpu.VMEM((256, HALF), BF16),
            pltpu.VMEM((320, 64), BF16),
            pltpu.VMEM((4, 8, 128), F32),
            pltpu.VMEM((16, 8, 128), F32),
            pltpu.VMEM((2, 16, 96, 128), BF16),
            pltpu.VMEM((NV, NV), BF16),
            pltpu.VMEM((NV, HALF), BF16),
            pltpu.VMEM((16, 96, 128), BF16),
            pltpu.VMEM((8, 96, 128), BF16),
            pltpu.VMEM((8, 96, 128), BF16),
            pltpu.VMEM((16, 96, 128), BF16),
            pltpu.VMEM((16, 8, 128), F32),
            pltpu.VMEM((8, 8, 128), F32),
            dma, dma((3,)),
            dma((16,)), dma,
            dma((16,)), dma((16,)), dma((2, 16)),
            dma((8,)), dma((8,)),
            dma((8,)), dma,
            dma((16,)), dma,
        ],
        compiler_params=pltpu.CompilerParams(
            collective_id=0, has_side_effects=True, vmem_limit_bytes=62 * 1024 * 1024
        ),
        cost_estimate=pl.CostEstimate(flops=3_060_000_000, bytes_accessed=2_700_000, transcendentals=0),
    )(amplitudes, cholesky, virt_irreps.reshape(9, 128), pair_irreps)


def solution(mesh):
    placed = (P("blk", None, "row"), P("blk", None, None), P(), P())
    return jax.shard_map(
        per_device, mesh=mesh, in_specs=placed, out_specs=P("blk", None, "row"), check_vma=False
    )
```

```python
import jax
import jax.numpy as jnp
from jax import lax
from jax.experimental import pallas as pl
from jax.experimental.pallas import tpu as pltpu
from jax.sharding import PartitionSpec as P

NV = 1152
BLK = 144
TILE = 18
HALF = 576
CHIP = 72
ROW4 = 288
F32 = jnp.float32
BF16 = jnp.bfloat16
I32 = jnp.int32
MESH = pl.DeviceIdType.MESH


def iota(shape, dim):
    return lax.broadcasted_iota(I32, shape, dim)


def dot(a, b):
    return jnp.dot(a, b, preferred_element_type=F32)


def dot_nt(a, b):
    return lax.dot_general(a, b, (((1,), (1,)), ((), ())), preferred_element_type=F32)


def lane_key(lane):
    main = ((lane >> 5) << 6) + (lane & 31)
    tail = (((lane >> 2) & 3) << 6) + 32 + (lane & 3)
    return jnp.where(lane < 128, main, tail)


def over36(v):
    return (v >= 36).astype(I32) + (v >= 72).astype(I32) + (v >= 108).astype(I32)


def kernel(
    amp_hbm, chol_ref, irr_hbm, pair_hbm, out_ref,
    amp_ref, irr9, pair_ref, irr_ref, vec, irrblk, rankblk, irrhalf, rankrow, rankhalf, colg, x32, own, rpack,
    lanek, expand, reduce_r, tailsel, tx1, rx1, gathered, texp, inner, outgoing,
    sibling, summed, rx3, tx4, rx4,
    vec_sem, small_sem, s1_send, s1_recv, s2_send, s2_fwd, s2_recv, s3_sib_send, s3_sib_recv,
    s3_send, s3_recv, s4_send, s4_recv,
):
    j = lax.axis_index("blk")
    r = lax.axis_index("row")
    m, zh, core = j // 4, (j // 2) % 2, j % 2
    x, y = m // 4, m % 4
    p, h = r % 4, 1 - r // 4
    z = 8 * zh + r
    other = 4 * m + 2 * zh + (1 - core)

    load_vec = pltpu.make_async_copy(chol_ref.at[0], vec, vec_sem)
    loads = [
        pltpu.make_async_copy(irr_hbm, irr9, small_sem.at[0]),
        pltpu.make_async_copy(pair_hbm, pair_ref, small_sem.at[1]),
        pltpu.make_async_copy(amp_hbm, amp_ref, small_sem.at[2]),
    ]
    for load in loads:
        load.start()
    load_vec.start()

    barrier = pltpu.get_barrier_semaphore()

    def ring_far(t):
        return 8 + (t // 2) * (1 - 2 * (t % 2)) - t % 2

    def greet_line(t, c):
        zd = (z + ring_far(t)) % 16
        for k in range(2):
            @pl.when(jnp.logical_or(t < 15, core != k))
            def _():
                pl.semaphore_signal(
                    barrier, inc=1, device_id=(4 * m + 2 * (zd // 8) + k, zd % 8), device_id_type=MESH
                )
        return c

    lax.fori_loop(0, 16, greet_line, 0)

    def far(i):
        return 2 + i // 2 - (i % 2) * (1 + 2 * (i // 2))

    def peer(o):
        return 4 * ((x + far(o % 4)) % 4) + (y + far(o // 4)) % 4

    def source(o):
        return 4 * ((x + 4 - far(o % 4)) % 4) + (y + 4 - far(o // 4)) % 4

    def greet_plane(o, c):
        pl.semaphore_signal(barrier, inc=1, device_id=(4 * peer(o) + 2 * zh + core, r), device_id_type=MESH)
        return c

    lax.fori_loop(0, 15, greet_plane, 0)

    for load in loads:
        load.wait()
    irr = jnp.concatenate([irr9[k : k + 1, :] for k in range(9)], axis=1)
    irr_ref[...] = irr
    upper = (iota((BLK, BLK), 0) < iota((BLK, BLK), 1)).astype(BF16)
    eye = iota((BLK, BLK), 0) == iota((BLK, BLK), 1)
    ones = jnp.ones((BLK, 128), BF16)
    pair_own = pair_ref[p]
    members = []
    for b in range(8):
        irr_b = irr[:, BLK * b : BLK * (b + 1)]
        irrblk[b : b + 1, :] = irr_b
        members.append((jnp.broadcast_to(irr_b, (8, BLK)) == iota((8, BLK), 0)).astype(F32))
        diagonal = jnp.where(eye, jnp.broadcast_to(irr_b, (BLK, BLK)), 0).astype(F32).astype(BF16)
        column = dot(diagonal, ones).astype(I32)
        colg[BLK * b : BLK * (b + 1), :] = jnp.bitwise_xor(column, pair_own)
    irrhalf[0:1, :] = irr[:, :HALF]
    irrhalf[1:2, :] = irr[:, HALF:]
    members = jnp.concatenate(members, axis=0)
    before = members * dot(members.astype(BF16), upper)
    for b in range(8):
        rank_b = jnp.sum(before[8 * b : 8 * b + 8], axis=0, keepdims=True).astype(I32)
        rankblk[b : b + 1, :] = rank_b
        keyed = rank_b + 64 * b
        rankrow[:, BLK * b : BLK * (b + 1)] = keyed
    rankhalf[0:1, :] = rankrow[:, :HALF]
    rankhalf[1:2, :] = rankrow[:, HALF:] - 256

    row72 = iota((CHIP, 1), 0)
    own_index = TILE * j + (row72 >> 2)
    own_irr = jnp.sum(
        jnp.where(iota((CHIP, NV), 1) == own_index, jnp.broadcast_to(irr, (CHIP, NV)), 0).astype(F32),
        axis=1, keepdims=True,
    ).astype(I32)
    pairs_col = jnp.zeros((CHIP, 1), I32)
    for q in range(4):
        pairs_col = jnp.where((row72 & 3) == q, pair_ref[q], pairs_col)
    own_goal = jnp.bitwise_xor(own_irr, pairs_col)
    own_mask = (own_goal == irrblk[pl.ds(r, 1), :]).astype(F32)
    own[...] = own_mask
    lane128 = iota((128, BLK), 0)
    slot128 = lane128 - 36 * over36(lane128)
    rpack[...] = jnp.logical_and(lane128 < 108, slot128 == rankblk[pl.ds(r, 1), :]).astype(BF16)
    for dd in range(TILE):
        x32[4 * dd : 4 * dd + 4, :] = amp_ref[dd].astype(F32)
    masked = (x32[...] * own_mask).astype(BF16)
    lane_group = over36(iota((CHIP, 128), 1))
    third = iota((CHIP, 128), 0)
    third = (third >= 24).astype(I32) + (third >= 48).astype(I32)
    spread = jnp.where(lane_group == third, dot_nt(masked, rpack[...]), 0.0).astype(BF16)
    pk_row, pk_col = iota((32, CHIP), 0), iota((32, CHIP), 1)
    col_third = (pk_col >= 24).astype(I32) + (pk_col >= 48).astype(I32)
    pick = jnp.logical_and(
        (pk_row >> 3) == (pk_col & 3), (pk_row & 7) == (pk_col >> 2) - 6 * col_third
    ).astype(BF16)
    packed = dot(pick, spread)
    for q in range(4):
        tx1[q] = packed[8 * q : 8 * q + 8]

    pl.semaphore_wait(barrier, 46)

    slot_me = (r % 4) * 4 + 2 * zh + core

    def s1_copy(t):
        zd = (z + ring_far(t)) % 16
        return pltpu.make_async_remote_copy(
            src_ref=tx1.at[zd % 4], dst_ref=rx1.at[slot_me],
            send_sem=s1_send.at[t], recv_sem=s1_recv,
            device_id=(4 * m + 2 * (zd // 8) + r // 4, zd % 8), device_id_type=MESH,
        )

    def s1_is_me(t):
        return jnp.logical_and(core == r // 4, t == 15)

    def s1_start(t, c):
        if t < 15:
            s1_copy(t).start()
            return c
        me = core == r // 4

        @pl.when(jnp.logical_not(me))
        def _():
            s1_copy(t).start()

        @pl.when(me)
        def _():
            pltpu.make_async_copy(tx1.at[p], rx1.at[slot_me], s1_recv).start()
        return c

    for t in range(16):
        s1_start(t, 0)

    col = iota((1, 768), 1)
    key = lane_key(col & 255)
    target = (key >> 6) * 128 + 36 * (col >> 8) + (key & 63)
    lanek[...] = (iota((512, 768), 0) == target).astype(BF16)
    lane_col = iota((512, 1), 0)
    expand[...] = (lane_key(lane_col & 255) + 256 * (lane_col >> 8) == rankrow[...]).astype(BF16)
    reduce_r[...] = (lane_key(iota((256, 1), 0)) == rankhalf[pl.ds(h, 1), :]).astype(BF16)
    ts_row, ts_col = iota((320, 64), 0), iota((320, 64), 1)
    tailsel[...] = jnp.logical_and(
        (ts_row >> 3) == 10 * (ts_col >> 4) + (ts_col & 15), (ts_col & 15) < 10
    ).astype(BF16)
    u_row, u_lane = iota((ROW4, 128), 0), iota((ROW4, 128), 1)
    u_match = (u_row & 7) == (u_lane >> 4)
    u_match320 = (iota((320, 128), 0) & 7) == (iota((320, 128), 1) >> 4)

    def row_target(c):
        return TILE * ((c >> 3) & 3) + 6 * (c >> 5) + (c & 7)

    rs_row, rs_col = iota((80, 96), 0), iota((80, 96), 1)
    rowsel = jnp.logical_and(rs_row == row_target(rs_col), (rs_col & 7) < 6).astype(BF16)
    rt_row, rt_col = iota((96, 80), 0), iota((96, 80), 1)
    rowsel_t = jnp.logical_and(rt_col == row_target(rt_row), (rt_row & 7) < 6).astype(BF16)
    rq_row, rq_col = iota((96, 16), 0), iota((96, 16), 1)
    rowsel_tail = jnp.logical_and(rq_col == row_target(rq_row) >> 3, (rq_row & 7) < 6).astype(BF16)
    row_u = (row_target(iota((96, 128), 0)) & 7) == (iota((96, 128), 1) >> 4)
    tail_pack = ((iota((16, 80), 1) >> 3) == iota((16, 80), 0)).astype(BF16)
    tp_row, tp_col = iota((64, ROW4), 0), iota((64, ROW4), 1)
    tail_pack4 = jnp.logical_and(
        (tp_col >> 3) == 9 * (tp_row >> 4) + (tp_row & 15), (tp_row & 15) < 9
    ).astype(BF16)

    pltpu.make_async_copy(rx1, rx1, s1_recv).wait()
    arrived = jnp.concatenate([rx1[s] for s in range(16)], axis=0)
    wide = jnp.concatenate([arrived[32 * g : 32 * g + 32] for g in range(4)], axis=1).astype(BF16)
    placed = dot(wide, lanek[...]).astype(BF16)
    stacked = jnp.concatenate([placed[:, 256 * k : 256 * k + 256] for k in range(3)], axis=0)
    rows = dot(rowsel, stacked)
    gathered[core, m, 0:80] = rows[:, :128].astype(BF16)
    tails = jnp.where(u_match320[:80], rows[:, 128:], 0.0).astype(BF16)
    gathered[core, m, 80:96] = dot(tail_pack, tails).astype(BF16)

    def s2_copy(o):
        return pltpu.make_async_remote_copy(
            src_ref=gathered.at[core, m], dst_ref=gathered.at[core, m],
            send_sem=s2_send.at[o], recv_sem=s2_recv.at[core, m],
            device_id=(4 * peer(o) + 2 * zh + core, r), device_id_type=MESH,
        )

    def s2_pass(o):
        src = source(o)
        return pltpu.make_async_remote_copy(
            src_ref=gathered.at[core, src], dst_ref=gathered.at[core, src],
            send_sem=s2_fwd.at[o], recv_sem=s2_recv.at[core, src],
            device_id=(other, r), device_id_type=MESH,
        )

    def arrival(part, src):
        return pltpu.make_async_copy(gathered.at[part, src], gathered.at[part, src], s2_recv.at[part, src])

    def s2_start(o, c):
        s2_copy(o).start()
        return c

    for o in range(15):
        s2_start(o, 0)
    s2_pass(15).start()

    def hand_on(o, c):
        arrival(core, source(o)).wait()
        s2_pass(o).start()
        return c

    lax.fori_loop(0, 15, hand_on, 0)
    load_vec.wait()

    def wait_sibling(o, c):
        arrival(1 - core, source(o)).wait()
        return c

    lax.fori_loop(0, 16, wait_sibling, 0)

    u_all = (iota((1280, 128), 0) & 7) == (iota((1280, 128), 1) >> 4)
    parts = []
    for half in range(2):
        main = jnp.concatenate([gathered[half, chip, 0:80] for chip in range(16)], axis=0)
        tail = jnp.concatenate([
            dot(tailsel[...], jnp.concatenate([gathered[half, 4 * g + k, 80:96] for k in range(4)], axis=0))
            for g in range(4)
        ], axis=0)
        tail = jnp.where(u_all, tail, 0.0).astype(BF16)
        parts.append(jnp.concatenate([main, tail], axis=1))

    def put(begin, end, value):
        value = jnp.concatenate([value[80 * k : 80 * k + CHIP] for k in range(16)], axis=0)
        wide_goal = jnp.concatenate([colg[...]] * ((end - begin) // 128), axis=1)
        keep = wide_goal == irr_ref[:, begin:end]
        texp[:, begin:end] = jnp.where(keep, value, 0.0).astype(BF16)

    put(0, 512, dot(parts[0], expand[0:256, 0:512]))
    put(512, 768, dot(jnp.concatenate(parts, axis=1), expand[:, 512:768]))
    put(768, 1152, dot(parts[1], expand[256:512, 768:1152]))
    rows_h = vec[pl.ds(pl.multiple_of(HALF * h, HALF), HALF), :]
    inner[...] = dot_nt(texp[...], rows_h).astype(BF16)

    def slot_of(d):
        return (d // 8) * 4 + d % 4

    def sib_copy(d):
        return pltpu.make_async_remote_copy(
            src_ref=outgoing.at[d], dst_ref=sibling.at[slot_of(d)],
            send_sem=s3_sib_send.at[slot_of(d)], recv_sem=s3_sib_recv.at[slot_of(d)],
            device_id=(other, r), device_id_type=MESH,
        )

    def s3_copy(d):
        return pltpu.make_async_remote_copy(
            src_ref=summed.at[slot_of(d)], dst_ref=rx3.at[m],
            send_sem=s3_send.at[slot_of(d)], recv_sem=s3_recv,
            device_id=(4 * d + 2 * zh + core, r), device_id_type=MESH,
        )

    def merge(xd):
        for k in range(4):
            d = 4 * xd + k
            slot = slot_of(d)
            pltpu.make_async_copy(sibling.at[slot], sibling.at[slot], s3_sib_recv.at[slot]).wait()
            total = (outgoing[d].astype(F32) + sibling[slot].astype(F32)).astype(BF16)

            @pl.when(d == m)
            def _():
                rx3[m] = total

            @pl.when(d != m)
            def _():
                summed[slot] = total
                s3_copy(d).start()

    def chunk_out(xd):
        first = pl.multiple_of(ROW4 * xd, ROW4)
        sig = dot(vec[pl.ds(first, ROW4), :], inner[...])
        goal = colg[pl.ds(first, ROW4), :]
        wide_goal = jnp.concatenate([goal] * 4 + [goal[:, :64]], axis=1)
        keep = wide_goal == irrhalf[pl.ds(h, 1), :]
        sig = jnp.where(keep, sig, 0.0).astype(BF16)
        short = dot_nt(sig, reduce_r[...])
        tail = jnp.where(u_match, short[:, 128:], 0.0).astype(BF16)
        tail = dot(tail_pack4, tail)
        for k in range(4):
            block = jnp.concatenate([short[CHIP * k : CHIP * k + CHIP, :128], jnp.zeros((8, 128), F32)], axis=0)
            outgoing[4 * xd + k, 0:80] = block.astype(BF16)
            outgoing[4 * xd + k, 80:96] = tail[16 * k : 16 * k + 16].astype(BF16)

    even = (x + core) % 2
    for k in range(2):
        xd = (x + 2 - 2 * k + 1 - even) % 4
        chunk_out(xd)
        for n in range(4):
            sib_copy(4 * xd + n).start()
    for k in range(2):
        xd = (x + 2 - 2 * k + even) % 4
        chunk_out(xd)
        merge(xd)

    def s4_copy(t):
        rr, tile = t // 4, t % 4
        return pltpu.make_async_remote_copy(
            src_ref=tx4.at[t], dst_ref=rx4.at[2 * p + zh],
            send_sem=s4_send.at[t], recv_sem=s4_recv,
            device_id=(4 * m + tile, 4 * h + rr), device_id_type=MESH,
        )

    reducer = core == x % 2

    @pl.when(reducer)
    def _():
        pltpu.make_async_copy(rx3.at[0:15], rx3.at[0:15], s3_recv).wait()
        total = rx3[0].astype(F32)
        for s in range(1, 16):
            total = total + rx3[s].astype(F32)
        total = total.astype(BF16)
        tail = jnp.where(row_u, dot(rowsel_tail, total[80:96]), 0.0).astype(BF16)
        by_row = jnp.concatenate([dot(rowsel_t, total[0:80]).astype(BF16), tail], axis=1)
        by_row = jnp.concatenate([by_row[32 * k : 32 * k + 32] for k in range(3)], axis=1)
        result = dot_nt(by_row, lanek[...])
        for t in range(16):
            tx4[t] = result[8 * (t % 4) : 8 * (t % 4) + 8, 128 * (t // 4) : 128 * (t // 4) + 128]

        def s4_start(t, c):
            zd = (z + ring_far(t)) % 16

            @pl.when((zd % 8) // 4 == h)
            def _():
                for k in range(2):
                    s4_copy(4 * (zd % 4) + 2 * (zd // 8) + k).start()
            return c

        for t in range(16):
            s4_start(t, 0)

    def s1_done(t, c):
        @pl.when(jnp.logical_not(s1_is_me(t)))
        def _():
            s1_copy(t).wait_send()
        return c

    lax.fori_loop(0, 16, s1_done, 0)
    s2_pass(15).wait_send()

    def s2_done(o, c):
        s2_copy(o).wait_send()
        s2_pass(o).wait_send()
        return c

    lax.fori_loop(0, 15, s2_done, 0)

    def s3_done(n, c):
        sib_copy(8 * (n // 4) + 4 * (1 - core) + n % 4).wait_send()
        d = 8 * (n // 4) + 4 * core + n % 4

        @pl.when(d != m)
        def _():
            s3_copy(d).wait_send()
        return c

    lax.fori_loop(0, 8, s3_done, 0)

    @pl.when(reducer)
    def _():
        def s4_done(t, c):
            s4_copy(t).wait_send()
            return c

        lax.fori_loop(0, 16, s4_done, 0)

    pltpu.make_async_copy(rx4, rx4, s4_recv).wait()
    got = jnp.concatenate([rx4[2 * q] + rx4[2 * q + 1] for q in range(4)], axis=0).astype(BF16)
    up_row, up_col = iota((CHIP, 32), 0), iota((CHIP, 32), 1)
    up_third = (up_row >= 24).astype(I32) + (up_row >= 48).astype(I32)
    unpick = jnp.logical_and(
        (up_col >> 3) == (up_row & 3), (up_col & 7) == (up_row >> 2) - 6 * up_third
    ).astype(BF16)
    spread_out = jnp.where(lane_group == third, dot(unpick, got), 0.0).astype(BF16)
    final = dot(spread_out, rpack[...]) * own[...]
    for dd in range(TILE):
        out_ref[dd] = final[4 * dd : 4 * dd + 4, :].astype(BF16)


def per_device(amplitudes, cholesky, virt_irreps, pair_irreps):
    vmem = pl.BlockSpec(memory_space=pltpu.VMEM)
    dma = pltpu.SemaphoreType.DMA
    return pl.pallas_call(
        kernel,
        out_shape=jax.ShapeDtypeStruct(amplitudes.shape, BF16),
        in_specs=[pl.BlockSpec(memory_space=pltpu.HBM)] * 4,
        out_specs=vmem,
        scratch_shapes=[
            pltpu.VMEM((TILE, 4, BLK), BF16),
            pltpu.VMEM((9, 128), I32),
            pltpu.SMEM((4,), I32),
            pltpu.VMEM((1, NV), I32),
            pltpu.VMEM((NV, NV), BF16),
            pltpu.VMEM((8, BLK), I32),
            pltpu.VMEM((8, BLK), I32),
            pltpu.VMEM((8, HALF), I32),
            pltpu.VMEM((1, NV), I32),
            pltpu.VMEM((8, HALF), I32),
            pltpu.VMEM((NV, 128), I32),
            pltpu.VMEM((CHIP, BLK), F32),
            pltpu.VMEM((CHIP, BLK), F32),
            pltpu.VMEM((128, BLK), BF16),
            pltpu.VMEM((512, 768), BF16),
            pltpu.VMEM((512, NV), BF16),
            pltpu.VMEM((256, HALF), BF16),
            pltpu.VMEM((320, 64), BF16),
            pltpu.VMEM((4, 8, 128), F32),
            pltpu.VMEM((16, 8, 128), F32),
            pltpu.VMEM((2, 16, 96, 128), BF16),
            pltpu.VMEM((NV, NV), BF16),
            pltpu.VMEM((NV, HALF), BF16),
            pltpu.VMEM((16, 96, 128), BF16),
            pltpu.VMEM((8, 96, 128), BF16),
            pltpu.VMEM((8, 96, 128), BF16),
            pltpu.VMEM((16, 96, 128), BF16),
            pltpu.VMEM((16, 8, 128), F32),
            pltpu.VMEM((8, 8, 128), F32),
            dma, dma((3,)),
            dma((16,)), dma,
            dma((16,)), dma((16,)), dma((2, 16)),
            dma((8,)), dma((8,)),
            dma((8,)), dma,
            dma((16,)), dma,
        ],
        compiler_params=pltpu.CompilerParams(
            collective_id=0, has_side_effects=True, vmem_limit_bytes=62 * 1024 * 1024
        ),
        cost_estimate=pl.CostEstimate(flops=3_060_000_000, bytes_accessed=2_700_000, transcendentals=0),
    )(amplitudes, cholesky, virt_irreps.reshape(9, 128), pair_irreps)


def solution(mesh):
    placed = (P("blk", None, "row"), P("blk", None, None), P(), P())
    return jax.shard_map(
        per_device, mesh=mesh, in_specs=placed, out_specs=P("blk", None, "row"), check_vma=False
    )
```

```python
import jax
import jax.numpy as jnp
from jax import lax
from jax.experimental import pallas as pl
from jax.experimental.pallas import tpu as pltpu
from jax.sharding import PartitionSpec as P

NV = 1152
BLK = 144
TILE = 18
HALF = 576
CHIP = 72
ROW4 = 288
F32 = jnp.float32
BF16 = jnp.bfloat16
I32 = jnp.int32
MESH = pl.DeviceIdType.MESH


def iota(shape, dim):
    return lax.broadcasted_iota(I32, shape, dim)


def dot(a, b):
    return jnp.dot(a, b, preferred_element_type=F32)


def dot_nt(a, b):
    return lax.dot_general(a, b, (((1,), (1,)), ((), ())), preferred_element_type=F32)


def lane_key(lane):
    main = ((lane >> 5) << 6) + (lane & 31)
    tail = (((lane >> 2) & 3) << 6) + 32 + (lane & 3)
    return jnp.where(lane < 128, main, tail)


def over36(v):
    return (v >= 36).astype(I32) + (v >= 72).astype(I32) + (v >= 108).astype(I32)


def kernel(
    amp_hbm, chol_ref, irr_hbm, pair_hbm, out_ref,
    amp_ref, irr9, pair_ref, irr_ref, vec, irrblk, rankblk, irrhalf, rankrow, rankhalf, colg, x32, own, rpack,
    vec_t, irrpad, lanek, expand, reduce_r, tailsel, tx1, rx1, gathered, texp, inner, outgoing,
    sibling, summed, rx3, tx4, rx4,
    vec_sem, small_sem, s1_send, s1_recv, s2_send, s2_fwd, s2_recv, s3_sib_send, s3_sib_recv,
    s3_send, s3_recv, s4_send, s4_recv,
):
    j = lax.axis_index("blk")
    r = lax.axis_index("row")
    m, zh, core = j // 4, (j // 2) % 2, j % 2
    x, y = m // 4, m % 4
    p, h = r % 4, 1 - r // 4
    z = 8 * zh + r
    other = 4 * m + 2 * zh + (1 - core)

    load_vec = pltpu.make_async_copy(chol_ref.at[0], vec, vec_sem)
    loads = [
        pltpu.make_async_copy(irr_hbm, irr9, small_sem.at[0]),
        pltpu.make_async_copy(pair_hbm, pair_ref, small_sem.at[1]),
        pltpu.make_async_copy(amp_hbm, amp_ref, small_sem.at[2]),
    ]
    for load in loads:
        load.start()
    load_vec.start()

    barrier = pltpu.get_barrier_semaphore()

    def ring_far(t):
        return 8 + (t // 2) * (1 - 2 * (t % 2)) - t % 2

    def greet_line(t, c):
        zd = (z + ring_far(t)) % 16
        for k in range(2):
            @pl.when(jnp.logical_or(t < 15, core != k))
            def _():
                pl.semaphore_signal(
                    barrier, inc=1, device_id=(4 * m + 2 * (zd // 8) + k, zd % 8), device_id_type=MESH
                )
        return c

    lax.fori_loop(0, 16, greet_line, 0)

    def far(i):
        return 2 + i // 2 - (i % 2) * (1 + 2 * (i // 2))

    def peer(o):
        return 4 * ((x + far(o % 4)) % 4) + (y + far(o // 4)) % 4

    def source(o):
        return 4 * ((x + 4 - far(o % 4)) % 4) + (y + 4 - far(o // 4)) % 4

    def greet_plane(o, c):
        pl.semaphore_signal(barrier, inc=1, device_id=(4 * peer(o) + 2 * zh + core, r), device_id_type=MESH)
        return c

    lax.fori_loop(0, 15, greet_plane, 0)

    for load in loads:
        load.wait()
    irr = jnp.concatenate([irr9[k : k + 1, :] for k in range(9)], axis=1)
    irr_ref[...] = irr
    upper = (iota((BLK, BLK), 0) < iota((BLK, BLK), 1)).astype(BF16)
    eye = iota((BLK, BLK), 0) == iota((BLK, BLK), 1)
    ones = jnp.ones((BLK, 128), BF16)
    pair_own = pair_ref[p]
    members = []
    for b in range(8):
        irr_b = irr[:, BLK * b : BLK * (b + 1)]
        irrblk[b : b + 1, :] = irr_b
        members.append((jnp.broadcast_to(irr_b, (8, BLK)) == iota((8, BLK), 0)).astype(F32))
        diagonal = jnp.where(eye, jnp.broadcast_to(irr_b, (BLK, BLK)), 0).astype(F32).astype(BF16)
        column = dot(diagonal, ones).astype(I32)
        colg[BLK * b : BLK * (b + 1), :] = jnp.bitwise_xor(column, pair_own)
    irrhalf[0:1, :] = irr[:, :HALF]
    irrhalf[1:2, :] = irr[:, HALF:]
    members = jnp.concatenate(members, axis=0)
    before = members * dot(members.astype(BF16), upper)
    for b in range(8):
        rank_b = jnp.sum(before[8 * b : 8 * b + 8], axis=0, keepdims=True).astype(I32)
        rankblk[b : b + 1, :] = rank_b
        keyed = rank_b + 64 * b
        rankrow[:, BLK * b : BLK * (b + 1)] = keyed
    rankhalf[0:1, :] = rankrow[:, :HALF]
    rankhalf[1:2, :] = rankrow[:, HALF:] - 256

    row72 = iota((CHIP, 1), 0)
    own_index = TILE * j + (row72 >> 2)
    own_irr = jnp.sum(
        jnp.where(iota((CHIP, NV), 1) == own_index, jnp.broadcast_to(irr, (CHIP, NV)), 0).astype(F32),
        axis=1, keepdims=True,
    ).astype(I32)
    pairs_col = jnp.zeros((CHIP, 1), I32)
    for q in range(4):
        pairs_col = jnp.where((row72 & 3) == q, pair_ref[q], pairs_col)
    own_goal = jnp.bitwise_xor(own_irr, pairs_col)
    own_mask = (own_goal == irrblk[pl.ds(r, 1), :]).astype(F32)
    own[...] = own_mask
    lane128 = iota((128, BLK), 0)
    slot128 = lane128 - 36 * over36(lane128)
    rpack[...] = jnp.logical_and(lane128 < 108, slot128 == rankblk[pl.ds(r, 1), :]).astype(BF16)
    for dd in range(TILE):
        x32[4 * dd : 4 * dd + 4, :] = amp_ref[dd].astype(F32)
    masked = (x32[...] * own_mask).astype(BF16)
    lane_group = over36(iota((CHIP, 128), 1))
    third = iota((CHIP, 128), 0)
    third = (third >= 24).astype(I32) + (third >= 48).astype(I32)
    spread = jnp.where(lane_group == third, dot_nt(masked, rpack[...]), 0.0).astype(BF16)
    pk_row, pk_col = iota((32, CHIP), 0), iota((32, CHIP), 1)
    col_third = (pk_col >= 24).astype(I32) + (pk_col >= 48).astype(I32)
    pick = jnp.logical_and(
        (pk_row >> 3) == (pk_col & 3), (pk_row & 7) == (pk_col >> 2) - 6 * col_third
    ).astype(BF16)
    packed = dot(pick, spread)
    for q in range(4):
        tx1[q] = packed[8 * q : 8 * q + 8]

    pl.semaphore_wait(barrier, 46)

    slot_me = (r % 4) * 4 + 2 * zh + core

    def s1_copy(t):
        zd = (z + ring_far(t)) % 16
        return pltpu.make_async_remote_copy(
            src_ref=tx1.at[zd % 4], dst_ref=rx1.at[slot_me],
            send_sem=s1_send.at[t], recv_sem=s1_recv,
            device_id=(4 * m + 2 * (zd // 8) + r // 4, zd % 8), device_id_type=MESH,
        )

    def s1_is_me(t):
        return jnp.logical_and(core == r // 4, t == 15)

    def s1_start(t, c):
        if t < 15:
            s1_copy(t).start()
            return c
        me = core == r // 4

        @pl.when(jnp.logical_not(me))
        def _():
            s1_copy(t).start()

        @pl.when(me)
        def _():
            pltpu.make_async_copy(tx1.at[p], rx1.at[slot_me], s1_recv).start()
        return c

    for t in range(16):
        s1_start(t, 0)

    col = iota((1, 768), 1)
    key = lane_key(col & 255)
    target = (key >> 6) * 128 + 36 * (col >> 8) + (key & 63)
    lanek[...] = (iota((512, 768), 0) == target).astype(BF16)
    empty = jnp.full((1, 64), -1, I32)
    for half in range(2):
        irrpad[half : half + 1, :] = jnp.concatenate([irrhalf[half : half + 1, :], empty], axis=1)
        keys = jnp.concatenate([rankhalf[half : half + 1, :], empty], axis=1)
        expand[half] = (lane_key(iota((256, 1), 0)) == keys).astype(BF16)
    reduce_r[...] = (lane_key(iota((256, 1), 0)) == rankhalf[pl.ds(h, 1), :]).astype(BF16)
    ts_row, ts_col = iota((320, 64), 0), iota((320, 64), 1)
    tailsel[...] = jnp.logical_and(
        (ts_row >> 3) == 10 * (ts_col >> 4) + (ts_col & 15), (ts_col & 15) < 10
    ).astype(BF16)
    u_row, u_lane = iota((ROW4, 128), 0), iota((ROW4, 128), 1)
    u_match = (u_row & 7) == (u_lane >> 4)
    u_match320 = (iota((320, 128), 0) & 7) == (iota((320, 128), 1) >> 4)

    def row_target(c):
        return TILE * ((c >> 3) & 3) + 6 * (c >> 5) + (c & 7)

    rs_row, rs_col = iota((80, 96), 0), iota((80, 96), 1)
    rowsel = jnp.logical_and(rs_row == row_target(rs_col), (rs_col & 7) < 6).astype(BF16)
    rt_row, rt_col = iota((96, 80), 0), iota((96, 80), 1)
    rowsel_t = jnp.logical_and(rt_col == row_target(rt_row), (rt_row & 7) < 6).astype(BF16)
    rq_row, rq_col = iota((96, 16), 0), iota((96, 16), 1)
    rowsel_tail = jnp.logical_and(rq_col == row_target(rq_row) >> 3, (rq_row & 7) < 6).astype(BF16)
    row_u = (row_target(iota((96, 128), 0)) & 7) == (iota((96, 128), 1) >> 4)
    tail_pack = ((iota((16, 80), 1) >> 3) == iota((16, 80), 0)).astype(BF16)
    tp_row, tp_col = iota((64, ROW4), 0), iota((64, ROW4), 1)
    tail_pack4 = jnp.logical_and(
        (tp_col >> 3) == 9 * (tp_row >> 4) + (tp_row & 15), (tp_row & 15) < 9
    ).astype(BF16)

    load_vec.wait()
    turned = vec[pl.ds(pl.multiple_of(HALF * h, HALF), HALF), :].T
    for half in range(2):
        vec_t[640 * half : 640 * half + HALF, :] = turned[HALF * half : HALF * half + HALF]
        vec_t[640 * half + HALF : 640 * half + 640, :] = jnp.zeros((64, HALF), BF16)
    pltpu.make_async_copy(rx1, rx1, s1_recv).wait()
    arrived = jnp.concatenate([rx1[s] for s in range(16)], axis=0)
    wide = jnp.concatenate([arrived[32 * g : 32 * g + 32] for g in range(4)], axis=1).astype(BF16)
    placed = dot(wide, lanek[...]).astype(BF16)
    stacked = jnp.concatenate([placed[:, 256 * k : 256 * k + 256] for k in range(3)], axis=0)
    rows = dot(rowsel, stacked)
    gathered[core, m, 0:80] = rows[:, :128].astype(BF16)
    tails = jnp.where(u_match320[:80], rows[:, 128:], 0.0).astype(BF16)
    gathered[core, m, 80:96] = dot(tail_pack, tails).astype(BF16)

    def s2_copy(o):
        return pltpu.make_async_remote_copy(
            src_ref=gathered.at[core, m], dst_ref=gathered.at[core, m],
            send_sem=s2_send.at[o], recv_sem=s2_recv.at[core, m],
            device_id=(4 * peer(o) + 2 * zh + core, r), device_id_type=MESH,
        )

    def s2_pass(o):
        src = source(o)
        return pltpu.make_async_remote_copy(
            src_ref=gathered.at[core, src], dst_ref=gathered.at[core, src],
            send_sem=s2_fwd.at[o], recv_sem=s2_recv.at[core, src],
            device_id=(other, r), device_id_type=MESH,
        )

    def arrival(part, src):
        return pltpu.make_async_copy(gathered.at[part, src], gathered.at[part, src], s2_recv.at[part, src])

    def s2_start(o, c):
        s2_copy(o).start()
        return c

    for o in range(15):
        s2_start(o, 0)
    s2_pass(15).start()

    def hand_on(o, c):
        arrival(core, source(o)).wait()
        s2_pass(o).start()
        return c

    lax.fori_loop(0, 15, hand_on, 0)

    def wait_sibling(o, c):
        arrival(1 - core, source(o)).wait()
        return c

    u_all = (iota((1280, 128), 0) & 7) == (iota((1280, 128), 1) >> 4)

    def spread_rows(half):
        main = jnp.concatenate([gathered[half, chip, 0:80] for chip in range(16)], axis=0)
        tail = jnp.concatenate([
            dot(tailsel[...], jnp.concatenate([gathered[half, 4 * g + k, 80:96] for k in range(4)], axis=0))
            for g in range(4)
        ], axis=0)
        tail = jnp.where(u_all, tail, 0.0).astype(BF16)
        value = dot(jnp.concatenate([main, tail], axis=1), expand[half])
        value = jnp.concatenate([value[80 * k : 80 * k + CHIP] for k in range(16)], axis=0)
        keep = jnp.concatenate([colg[...]] * 5, axis=1) == irrpad[pl.ds(half, 1), :]
        texp[:, pl.ds(pl.multiple_of(640 * half, 128), 640)] = jnp.where(keep, value, 0.0).astype(BF16)

    spread_rows(core)
    lax.fori_loop(0, 16, wait_sibling, 0)
    spread_rows(1 - core)
    inner[...] = dot(texp[...], vec_t[...]).astype(BF16)

    def slot_of(d):
        return (d // 8) * 4 + d % 4

    def sib_copy(d):
        return pltpu.make_async_remote_copy(
            src_ref=outgoing.at[d], dst_ref=sibling.at[slot_of(d)],
            send_sem=s3_sib_send.at[slot_of(d)], recv_sem=s3_sib_recv.at[slot_of(d)],
            device_id=(other, r), device_id_type=MESH,
        )

    def s3_copy(d):
        return pltpu.make_async_remote_copy(
            src_ref=summed.at[slot_of(d)], dst_ref=rx3.at[m],
            send_sem=s3_send.at[slot_of(d)], recv_sem=s3_recv,
            device_id=(4 * d + 2 * zh + core, r), device_id_type=MESH,
        )

    def merge(xd):
        for k in range(4):
            d = 4 * xd + k
            slot = slot_of(d)
            pltpu.make_async_copy(sibling.at[slot], sibling.at[slot], s3_sib_recv.at[slot]).wait()
            total = (outgoing[d].astype(F32) + sibling[slot].astype(F32)).astype(BF16)

            @pl.when(d == m)
            def _():
                rx3[m] = total

            @pl.when(d != m)
            def _():
                summed[slot] = total
                s3_copy(d).start()

    def chunk_out(xd):
        first = pl.multiple_of(ROW4 * xd, ROW4)
        sig = dot(vec[pl.ds(first, ROW4), :], inner[...])
        goal = colg[pl.ds(first, ROW4), :]
        wide_goal = jnp.concatenate([goal] * 4 + [goal[:, :64]], axis=1)
        keep = wide_goal == irrhalf[pl.ds(h, 1), :]
        sig = jnp.where(keep, sig, 0.0).astype(BF16)
        short = dot_nt(sig, reduce_r[...])
        tail = jnp.where(u_match, short[:, 128:], 0.0).astype(BF16)
        tail = dot(tail_pack4, tail)
        for k in range(4):
            block = jnp.concatenate([short[CHIP * k : CHIP * k + CHIP, :128], jnp.zeros((8, 128), F32)], axis=0)
            outgoing[4 * xd + k, 0:80] = block.astype(BF16)
            outgoing[4 * xd + k, 80:96] = tail[16 * k : 16 * k + 16].astype(BF16)

    even = (x + core) % 2
    for k in range(2):
        xd = (x + 2 - 2 * k + 1 - even) % 4
        chunk_out(xd)
        for n in range(4):
            sib_copy(4 * xd + n).start()
    for k in range(2):
        xd = (x + 2 - 2 * k + even) % 4
        chunk_out(xd)
        merge(xd)

    def s4_copy(t):
        rr, tile = t // 4, t % 4
        return pltpu.make_async_remote_copy(
            src_ref=tx4.at[t], dst_ref=rx4.at[2 * p + zh],
            send_sem=s4_send.at[t], recv_sem=s4_recv,
            device_id=(4 * m + tile, 4 * h + rr), device_id_type=MESH,
        )

    reducer = core == x % 2

    @pl.when(reducer)
    def _():
        pltpu.make_async_copy(rx3.at[0:15], rx3.at[0:15], s3_recv).wait()
        total = rx3[0].astype(F32)
        for s in range(1, 16):
            total = total + rx3[s].astype(F32)
        total = total.astype(BF16)
        tail = jnp.where(row_u, dot(rowsel_tail, total[80:96]), 0.0).astype(BF16)
        by_row = jnp.concatenate([dot(rowsel_t, total[0:80]).astype(BF16), tail], axis=1)
        by_row = jnp.concatenate([by_row[32 * k : 32 * k + 32] for k in range(3)], axis=1)
        result = dot_nt(by_row, lanek[...])
        for t in range(16):
            tx4[t] = result[8 * (t % 4) : 8 * (t % 4) + 8, 128 * (t // 4) : 128 * (t // 4) + 128]

        def s4_start(t, c):
            zd = (z + ring_far(t)) % 16

            @pl.when((zd % 8) // 4 == h)
            def _():
                for k in range(2):
                    s4_copy(4 * (zd % 4) + 2 * (zd // 8) + k).start()
            return c

        for t in range(16):
            s4_start(t, 0)

    def s1_done(t, c):
        @pl.when(jnp.logical_not(s1_is_me(t)))
        def _():
            s1_copy(t).wait_send()
        return c

    lax.fori_loop(0, 16, s1_done, 0)
    s2_pass(15).wait_send()

    def s2_done(o, c):
        s2_copy(o).wait_send()
        s2_pass(o).wait_send()
        return c

    lax.fori_loop(0, 15, s2_done, 0)

    def s3_done(n, c):
        sib_copy(8 * (n // 4) + 4 * (1 - core) + n % 4).wait_send()
        d = 8 * (n // 4) + 4 * core + n % 4

        @pl.when(d != m)
        def _():
            s3_copy(d).wait_send()
        return c

    lax.fori_loop(0, 8, s3_done, 0)

    @pl.when(reducer)
    def _():
        def s4_done(t, c):
            s4_copy(t).wait_send()
            return c

        lax.fori_loop(0, 16, s4_done, 0)

    pltpu.make_async_copy(rx4, rx4, s4_recv).wait()
    got = jnp.concatenate([rx4[2 * q] + rx4[2 * q + 1] for q in range(4)], axis=0).astype(BF16)
    up_row, up_col = iota((CHIP, 32), 0), iota((CHIP, 32), 1)
    up_third = (up_row >= 24).astype(I32) + (up_row >= 48).astype(I32)
    unpick = jnp.logical_and(
        (up_col >> 3) == (up_row & 3), (up_col & 7) == (up_row >> 2) - 6 * up_third
    ).astype(BF16)
    spread_out = jnp.where(lane_group == third, dot(unpick, got), 0.0).astype(BF16)
    final = dot(spread_out, rpack[...]) * own[...]
    for dd in range(TILE):
        out_ref[dd] = final[4 * dd : 4 * dd + 4, :].astype(BF16)


def per_device(amplitudes, cholesky, virt_irreps, pair_irreps):
    vmem = pl.BlockSpec(memory_space=pltpu.VMEM)
    dma = pltpu.SemaphoreType.DMA
    return pl.pallas_call(
        kernel,
        out_shape=jax.ShapeDtypeStruct(amplitudes.shape, BF16),
        in_specs=[pl.BlockSpec(memory_space=pltpu.HBM)] * 4,
        out_specs=vmem,
        scratch_shapes=[
            pltpu.VMEM((TILE, 4, BLK), BF16),
            pltpu.VMEM((9, 128), I32),
            pltpu.SMEM((4,), I32),
            pltpu.VMEM((1, NV), I32),
            pltpu.VMEM((NV, NV), BF16),
            pltpu.VMEM((8, BLK), I32),
            pltpu.VMEM((8, BLK), I32),
            pltpu.VMEM((8, HALF), I32),
            pltpu.VMEM((1, NV), I32),
            pltpu.VMEM((8, HALF), I32),
            pltpu.VMEM((NV, 128), I32),
            pltpu.VMEM((CHIP, BLK), F32),
            pltpu.VMEM((CHIP, BLK), F32),
            pltpu.VMEM((128, BLK), BF16),
            pltpu.VMEM((1280, HALF), BF16),
            pltpu.VMEM((8, 640), I32),
            pltpu.VMEM((512, 768), BF16),
            pltpu.VMEM((2, 256, 640), BF16),
            pltpu.VMEM((256, HALF), BF16),
            pltpu.VMEM((320, 64), BF16),
            pltpu.VMEM((4, 8, 128), F32),
            pltpu.VMEM((16, 8, 128), F32),
            pltpu.VMEM((2, 16, 96, 128), BF16),
            pltpu.VMEM((NV, 1280), BF16),
            pltpu.VMEM((NV, HALF), BF16),
            pltpu.VMEM((16, 96, 128), BF16),
            pltpu.VMEM((8, 96, 128), BF16),
            pltpu.VMEM((8, 96, 128), BF16),
            pltpu.VMEM((16, 96, 128), BF16),
            pltpu.VMEM((16, 8, 128), F32),
            pltpu.VMEM((8, 8, 128), F32),
            dma, dma((3,)),
            dma((16,)), dma,
            dma((16,)), dma((16,)), dma((2, 16)),
            dma((8,)), dma((8,)),
            dma((8,)), dma,
            dma((16,)), dma,
        ],
        compiler_params=pltpu.CompilerParams(
            collective_id=0, has_side_effects=True, vmem_limit_bytes=62 * 1024 * 1024
        ),
        cost_estimate=pl.CostEstimate(flops=3_060_000_000, bytes_accessed=2_700_000, transcendentals=0),
    )(amplitudes, cholesky, virt_irreps.reshape(9, 128), pair_irreps)


def solution(mesh):
    placed = (P("blk", None, "row"), P("blk", None, None), P(), P())
    return jax.shard_map(
        per_device, mesh=mesh, in_specs=placed, out_specs=P("blk", None, "row"), check_vma=False
    )
```
